32 devices in a mesh: grp: 2 (over y), seq: 16 (over z, x, core).
Axes of the slice: x: 2, y: 2, z: 4, core: 2. Of those that a mesh axis runs over, the one named last changes fastest.
Arguments:
- queries: bfloat16 [4096, 4096], P(('grp', 'seq')), parts along dimension 0, may hold values from -4.5 to 4.5
- kv_pool: bfloat16 [288, 8, 1024], P(('grp', 'seq')), parts along dimension 0, may hold values from -4.5 to 4.5
- span_lengths: int32 [32], P('grp'), parts along dimension 0, may hold values from 0 to 128, as said below
- owner_branch: int32 [32], P('grp'), parts along dimension 0, may hold values from 0 to 15, as said below
- prefix_table: int32 [256], P('grp'), parts along dimension 0, may hold values from 0 to 143, as said below
- branch_table: int32 [32, 1], P('grp'), parts along dimension 0, may hold values from 0 to 143, as said below
Outputs:
- attended: bfloat16 [4096, 4096], P(('grp', 'seq')), parts along dimension 0
The draws below stay inside these ranges and needn't reach their ends.
There are 2 independent parts, one for each index of `grp`. The reference program is written for one: setup_inputs(seed, part) draws one part's arguments, and reference() takes and returns one part's arrays. A program takes and returns all parts, laid end to end along the dimension named above; each array names one. Nothing has to cross between parts.
Inputs may be any that keep to these rules, and one draw needn't show every extreme that they name: `span_lengths`: the span lengths sum to 1024, and some branch has exactly 128 rows. `owner_branch`: A permutation of the branches. `prefix_table`: together with branch_table it names every page of the pool exactly once. `branch_table`: together with prefix_table it names every page of the pool exactly once.
All inputs are finite; a program needn't handle non-finite values.
Results may differ from the reference program's by a relative error of at most 0.008.
Values may be sent and summed in bfloat16 or wider, within the bound.
No kernel may reach another device: no remote copies, remote signals or barrier semaphores. Data moves between devices by JAX's collectives and lax.ppermute only.
A program may use at most 128 MiB of HBM per device.

```python
import math
import jax
import jax.numpy as jnp
from jax import lax

QH = 32
KVH = 4
HD = 128
BRANCHES = 16
PAGE = 8
MOST = 128
TOTAL_ROWS = 2048
PREFIX_PAGES = 128
HIST = 1
POOL = 144


def page_order(key):
    return jax.random.permutation(jax.random.fold_in(key, 601), POOL)


def draw_queries(key, part):
    key = jax.random.fold_in(key, 3)
    values = jnp.clip(jax.random.normal(key, (TOTAL_ROWS, QH * HD), jnp.float32), -4.5, 4.5)
    return values.astype(jnp.bfloat16)


def draw_kv_pool(key, part):
    key = jax.random.fold_in(key, 5)
    shape = (POOL, PAGE, 2 * KVH * HD)
    values = jnp.clip(jax.random.normal(key, shape, jnp.float32), -4.5, 4.5)
    return values.astype(jnp.bfloat16)


def draw_span_lengths(key, part):
    key = jax.random.fold_in(key, 7)
    half_most = MOST // 2
    offsets = jax.random.randint(jax.random.fold_in(key, 1), (BRANCHES // 2,), 0, half_most + 1)
    offsets = offsets.at[0].set(half_most)
    paired = jnp.stack([half_most + offsets, half_most - offsets], 1).reshape(BRANCHES)
    shuffle = jax.random.permutation(jax.random.fold_in(key, 2), BRANCHES)
    return paired[shuffle].astype(jnp.int32)


def draw_owner_branch(key, part):
    key = jax.random.fold_in(key, 11)
    return jax.random.permutation(key, BRANCHES).astype(jnp.int32)


def draw_prefix_table(key, part):
    order = page_order(key)
    return order[:PREFIX_PAGES].astype(jnp.int32)


def draw_branch_table(key, part):
    order = page_order(key)
    return order[PREFIX_PAGES:].reshape(BRANCHES, HIST).astype(jnp.int32)


def setup_inputs(seed: int = 0, part: int = 0) -> dict:
    key_of = jax.random.split(jax.random.key(seed), 7)
    own_keys = jax.random.split(jax.random.fold_in(key_of[6], part), 7)
    return {
        "queries": draw_queries(jax.random.fold_in(jax.random.fold_in(key_of[6], part), 71), part),
        "kv_pool": draw_kv_pool(jax.random.fold_in(jax.random.fold_in(key_of[6], part), 71), part),
        "span_lengths": draw_span_lengths(jax.random.fold_in(jax.random.fold_in(key_of[6], part), 71), part),
        "owner_branch": draw_owner_branch(jax.random.fold_in(jax.random.fold_in(key_of[6], part), 71), part),
        "prefix_table": draw_prefix_table(jax.random.fold_in(jax.random.fold_in(key_of[6], part), 71), part),
        "branch_table": draw_branch_table(jax.random.fold_in(jax.random.fold_in(key_of[6], part), 71), part),
    }


def branch_attention(query_block, branch, kv_pool, prefix_table, branch_table, span_lengths):
    pages = jnp.concatenate([kv_pool[prefix_table], kv_pool[branch_table[branch]]], 0)
    tokens = pages.reshape(-1, 2, KVH, HD)
    keys_all = jnp.transpose(tokens[:, 0], (1, 0, 2))
    values_all = jnp.transpose(tokens[:, 1], (1, 0, 2))
    heads_all = jnp.transpose(query_block.reshape(-1, KVH, QH // KVH, HD), (1, 0, 2, 3))

    def one_head(inputs):
        heads, keys, values = inputs
        heads = heads.astype(jnp.float32)
        keys = keys.astype(jnp.float32)
        values = values.astype(jnp.float32)
        scores = jnp.einsum('rgd,td->rgt', heads, keys) * (1.0 / math.sqrt(HD))
        row_max = lax.optimization_barrier(jnp.max(scores, -1))
        weights = jnp.exp(scores - row_max[..., None]).astype(jnp.bfloat16)
        totals = lax.optimization_barrier(jnp.sum(weights.astype(jnp.float32), -1))
        return jnp.einsum('rgt,td->rgd', weights.astype(jnp.float32), values) / totals[..., None]
    mixed = lax.map(one_head, (heads_all, keys_all, values_all))
    mixed = jnp.transpose(mixed, (1, 0, 2, 3)).reshape(-1, QH * HD)
    live_rows = jnp.arange(MOST, dtype=jnp.int32) < span_lengths[branch]
    return jnp.where(live_rows[:, None], mixed, 0.0).astype(jnp.bfloat16)

def reference(queries, kv_pool, span_lengths, owner_branch, prefix_table, branch_table):
    query_groups = queries.reshape(BRANCHES, MOST, QH * HD)

    def one_group(inputs):
        query_block, group_index = inputs
        branch = owner_branch[group_index]
        return branch_attention(query_block, branch, kv_pool, prefix_table, branch_table, span_lengths)
    outputs = lax.map(one_group, (query_groups, jnp.arange(BRANCHES, dtype=jnp.int32)))
    return outputs.reshape(TOTAL_ROWS, QH * HD)
```

```python
import functools
import math

import jax
import jax.numpy as jnp
from jax import lax
from jax.experimental import pallas as pl
from jax.experimental.pallas import tpu as pltpu
from jax.sharding import PartitionSpec as P

QH = 32
KVH = 4
HD = 128
GROUP = QH // KVH
EXP2_SCALE = math.log2(math.e) / math.sqrt(HD)
GATHER_DEVICES = 16


def page_owners(prefix_table, branch_table, pool_size):
    page_ids = jnp.arange(pool_size, dtype=jnp.int32)
    is_prefix = jnp.any(prefix_table[:, None] == page_ids[None, :], 0)
    flat_table = branch_table.reshape(-1)
    table_branch = jnp.arange(flat_table.shape[0], dtype=jnp.int32) // branch_table.shape[1]
    owner_of = jnp.sum(
        jnp.where(flat_table[:, None] == page_ids[None, :], table_branch[:, None], 0), 0
    )
    return jnp.where(is_prefix, -1, owner_of)


def absorb(carry, query_heads, pages, block_allowed):
    run_max, run_total, run_acc = carry
    page_tokens = pages.shape[1]
    token_count = pages.shape[0] * page_tokens
    kv_tokens = pages.reshape(token_count, 2, KVH, HD)
    keys = kv_tokens[:, 0]
    values = kv_tokens[:, 1]
    scores = jnp.einsum("rkgd,tkd->rkgt", query_heads, keys, preferred_element_type=jnp.float32) * (
        1.0 / math.sqrt(HD)
    )
    allowed = jnp.repeat(block_allowed, page_tokens)[None, None, None, :]
    masked = jnp.where(allowed, scores, -1e30)
    new_max = jnp.maximum(run_max, jnp.max(masked, -1))
    weights = jnp.where(allowed, jnp.exp(scores - new_max[..., None]), 0.0).astype(jnp.bfloat16)
    factor = jnp.exp(run_max - new_max)
    new_total = run_total * factor + jnp.sum(weights.astype(jnp.float32), -1)
    new_acc = run_acc * factor[..., None] + jnp.einsum(
        "rkgt,tkd->rkgd", weights, values, preferred_element_type=jnp.float32
    )
    return (new_max, new_total, new_acc)


def attend_general(queries, kv_pool, page_allowed, live_count):
    row_count = queries.shape[0]
    pages = lax.all_gather(kv_pool, "seq", axis=0, tiled=True)
    page_tokens = pages.shape[1]
    block_pages = max(1, max(128, 32768 // row_count) // page_tokens)
    while pages.shape[0] % block_pages:
        block_pages = block_pages - 1
    blocks = pages.reshape((-1, block_pages) + pages.shape[1:])
    block_allowed = page_allowed.reshape(-1, block_pages)
    query_heads = queries.reshape(row_count, KVH, GROUP, HD)
    start = (
        jnp.full((row_count, KVH, GROUP), -1e30, jnp.float32),
        jnp.zeros((row_count, KVH, GROUP), jnp.float32),
        jnp.zeros((row_count, KVH, GROUP, HD), jnp.float32),
    )

    def scan_step(state, inputs):
        block, allowed = inputs
        return (absorb(state, query_heads, block, allowed), None)

    (run_max, run_total, run_acc), unused = lax.scan(scan_step, start, (blocks, block_allowed))
    mixed = (run_acc / run_total[..., None]).reshape(row_count, QH * HD)
    live = jnp.arange(row_count, dtype=jnp.int32) < live_count
    return jnp.where(live[:, None], mixed, 0.0).astype(jnp.bfloat16)


def place(z, x, core):
    return z * 4 + x * 2 + core


def permute(block, target):
    pairs = []
    for index in range(GATHER_DEVICES):
        to = target(index // 4, index // 2 % 2, index % 2)
        if to is not None:
            pairs.append((index, place(*to)))
    return lax.ppermute(block, "seq", pairs)


def gather_pieces(shard):
    along_z = [
        shard,
        permute(shard, lambda z, x, c: (z ^ 1, x, c)),
        permute(shard, lambda z, x, c: (z ^ 2, x, c)),
        permute(shard, lambda z, x, c: (z ^ 3, x, c)),
    ]
    pieces = []
    for block in along_z:
        other = permute(block, lambda z, x, c: (z, 1 - x, c))
        for held in (block, other):
            pieces.append(held)
            pieces.append(permute(held, lambda z, x, c: (z, x, 1 - c)))
    return pieces


def attention_kernel(q_ref, bias_ref, live_ref, *refs, count):
    piece_refs = refs[:count]
    out_ref, keys, values = refs[count:]
    rows = q_ref.shape[0]
    tokens = keys.shape[1]
    piece = tokens // count
    values[:, :, HD:] = jnp.ones((KVH, tokens, HD), jnp.bfloat16)
    for i in range(count):
        block = piece_refs[i][...].reshape(piece, 2 * KVH * HD)
        span = slice(i * piece, (i + 1) * piece)
        for h in range(KVH):
            keys[h, span, :] = block[:, h * HD : (h + 1) * HD]
            values[h, span, :HD] = block[:, (KVH + h) * HD : (KVH + h + 1) * HD]
    live = lax.broadcasted_iota(jnp.int32, (rows, HD), 0) < live_ref[0]
    bias = bias_ref[...]
    for q_head in range(QH):
        h = q_head // GROUP
        lanes = slice(q_head * HD, (q_head + 1) * HD)
        scores = lax.dot_general(
            q_ref[:, lanes], keys[h], (((1,), (1,)), ((), ())), preferred_element_type=jnp.float32
        )
        scores = scores + bias
        row_max = jnp.max(scores, -1, keepdims=True)
        weights = jnp.exp2((scores - row_max) * EXP2_SCALE).astype(jnp.bfloat16)
        sums = jnp.dot(weights, values[h], preferred_element_type=jnp.float32)
        mixed = sums[:, :HD] / sums[:, HD:]
        out_ref[:, lanes] = jnp.where(live, mixed, 0.0).astype(jnp.bfloat16)


def attend_pieces(queries, pieces, bias, live_count):
    rows, features = queries.shape
    count = len(pieces)
    tokens = bias.shape[1]
    vmem = pl.BlockSpec(memory_space=pltpu.VMEM)
    return pl.pallas_call(
        functools.partial(attention_kernel, count=count),
        out_shape=jax.ShapeDtypeStruct((rows, features), jnp.bfloat16),
        in_specs=[vmem, vmem, pl.BlockSpec(memory_space=pltpu.SMEM)] + [vmem] * count,
        out_specs=vmem,
        scratch_shapes=[
            pltpu.VMEM((KVH, tokens, HD), jnp.bfloat16),
            pltpu.VMEM((KVH, tokens, 2 * HD), jnp.bfloat16),
        ],
        compiler_params=pltpu.CompilerParams(vmem_limit_bytes=40 << 20),
        cost_estimate=pl.CostEstimate(
            flops=4 * rows * features * tokens,
            bytes_accessed=4 * rows * features + 2 * tokens * KVH * HD * 2,
            transcendentals=rows * QH * tokens,
        ),
        name="attention",
    )(queries, bias, live_count.reshape(1), *pieces)


def per_device(queries, kv_pool, span_lengths, owner_branch, prefix_table, branch_table):
    device_count = lax.axis_size("seq")
    self_index = lax.axis_index("seq")
    capacity = queries.shape[0]
    branch_count = span_lengths.shape[0]
    owner_width = device_count // branch_count
    pages_dev, page_tokens = kv_pool.shape[:2]
    my_branch = owner_branch[self_index // owner_width]
    live_count = span_lengths[my_branch] - self_index % owner_width * capacity
    slot_branch = page_owners(prefix_table, branch_table, pages_dev * device_count)
    page_allowed = (slot_branch < 0) | (slot_branch == my_branch)
    if device_count != GATHER_DEVICES:
        return attend_general(queries, kv_pool, page_allowed, live_count)
    by_piece = page_allowed.reshape(device_count, pages_dev)[
        self_index ^ jnp.arange(device_count, dtype=jnp.int32)
    ]
    bias = jnp.where(jnp.repeat(by_piece.reshape(-1), page_tokens), 0.0, -1e30)[None, :]
    pieces = gather_pieces(kv_pool)
    return attend_pieces(queries, pieces, bias, live_count)


def solution(mesh):
    return jax.shard_map(
        per_device,
        mesh=mesh,
        in_specs=(
            P(("grp", "seq"), None),
            P(("grp", "seq"), None, None),
            P("grp"),
            P("grp"),
            P("grp"),
            P("grp", None),
        ),
        out_specs=P(("grp", "seq"), None),
        check_vma=False,
    )
```

```python
import functools
import math

import jax
import jax.numpy as jnp
from jax import lax
from jax.experimental import pallas as pl
from jax.experimental.pallas import tpu as pltpu
from jax.sharding import PartitionSpec as P

QH = 32
KVH = 4
HD = 128
GROUP = QH // KVH
EXP2_SCALE = math.log2(math.e) / math.sqrt(HD)
GATHER_DEVICES = 16
MASKED = -1e30


def page_owners(prefix_table, branch_table, pool_size):
    page_ids = jnp.arange(pool_size, dtype=jnp.int32)
    is_prefix = jnp.any(prefix_table[:, None] == page_ids[None, :], 0)
    flat_table = branch_table.reshape(-1)
    table_branch = jnp.arange(flat_table.shape[0], dtype=jnp.int32) // branch_table.shape[1]
    owner_of = jnp.sum(
        jnp.where(flat_table[:, None] == page_ids[None, :], table_branch[:, None], 0), 0
    )
    return jnp.where(is_prefix, -1, owner_of)


def absorb(carry, query_heads, pages, block_allowed):
    run_max, run_total, run_acc = carry
    page_tokens = pages.shape[1]
    token_count = pages.shape[0] * page_tokens
    kv_tokens = pages.reshape(token_count, 2, KVH, HD)
    keys = kv_tokens[:, 0]
    values = kv_tokens[:, 1]
    scores = jnp.einsum("rkgd,tkd->rkgt", query_heads, keys, preferred_element_type=jnp.float32) * (
        1.0 / math.sqrt(HD)
    )
    allowed = jnp.repeat(block_allowed, page_tokens)[None, None, None, :]
    masked = jnp.where(allowed, scores, -1e30)
    new_max = jnp.maximum(run_max, jnp.max(masked, -1))
    weights = jnp.where(allowed, jnp.exp(scores - new_max[..., None]), 0.0).astype(jnp.bfloat16)
    factor = jnp.exp(run_max - new_max)
    new_total = run_total * factor + jnp.sum(weights.astype(jnp.float32), -1)
    new_acc = run_acc * factor[..., None] + jnp.einsum(
        "rkgt,tkd->rkgd", weights, values, preferred_element_type=jnp.float32
    )
    return (new_max, new_total, new_acc)


def attend_general(queries, kv_pool, page_allowed, live_count):
    row_count = queries.shape[0]
    pages = lax.all_gather(kv_pool, "seq", axis=0, tiled=True)
    page_tokens = pages.shape[1]
    block_pages = max(1, max(128, 32768 // row_count) // page_tokens)
    while pages.shape[0] % block_pages:
        block_pages = block_pages - 1
    blocks = pages.reshape((-1, block_pages) + pages.shape[1:])
    block_allowed = page_allowed.reshape(-1, block_pages)
    query_heads = queries.reshape(row_count, KVH, GROUP, HD)
    start = (
        jnp.full((row_count, KVH, GROUP), -1e30, jnp.float32),
        jnp.zeros((row_count, KVH, GROUP), jnp.float32),
        jnp.zeros((row_count, KVH, GROUP, HD), jnp.float32),
    )

    def scan_step(state, inputs):
        block, allowed = inputs
        return (absorb(state, query_heads, block, allowed), None)

    (run_max, run_total, run_acc), unused = lax.scan(scan_step, start, (blocks, block_allowed))
    mixed = (run_acc / run_total[..., None]).reshape(row_count, QH * HD)
    live = jnp.arange(row_count, dtype=jnp.int32) < live_count
    return jnp.where(live[:, None], mixed, 0.0).astype(jnp.bfloat16)


MOVES = {"core": 1, "x": 2, "z1": 4, "z2": 8}
PLAN = (
    ("z2", 0, ()),
    ("z1", 0, ()),
    ("x", 0, ()),
    ("core", 0, ()),
    ("prepare", ()),
    ("x", 4, ("prepare",)),
    ("z1", 8, ()),
    ("x", 8, ()),
    ("x", 12, ()),
    ("core", 2, ()),
    ("core", 4, ()),
    ("core", 6, ()),
    ("core", 8, ()),
    ("core", 10, ()),
    ("core", 12, ()),
    ("attend", (0, 1, 2, 3, 4, 5, 6, 7), ()),
    ("core", 14, ("attend1",)),
    ("attend", (8, 9, 10, 11, 12, 13, 14, 15), ()),
)


def permute(block, move):
    pairs = [(index, index ^ MOVES[move]) for index in range(GATHER_DEVICES)]
    return lax.ppermute(block, "seq", pairs)


def after(value, *earlier):
    return lax.optimization_barrier((value,) + earlier)[0] if earlier else value


def prepare_kernel(
    q_ref, shard_ref, lengths_in, owner_in, table_in, q_out, shard_out, live_ref, *rest, stages
):
    bias_refs, (lengths_ref, owner_ref, table_ref, sems) = rest[:-4], rest[-4:]
    ends = (
        (lengths_in, lengths_ref),
        (owner_in, owner_ref),
        (table_in, table_ref),
        (q_ref, q_out),
        (shard_ref, shard_out),
    )
    copies = [pltpu.make_async_copy(*pair, sems.at[i]) for i, pair in enumerate(ends)]
    for copy in copies:
        copy.start()
    for copy in copies[:3]:
        copy.wait()
    pages_dev, page_tokens = shard_ref.shape[:2]
    me = lax.axis_index("seq")
    rows = q_ref.shape[0]
    owner_width = GATHER_DEVICES // owner_ref.shape[0]
    branch = owner_ref[me // owner_width]
    live_count = lengths_ref[branch] - me % owner_width * rows
    live_ref[...] = jnp.where(
        lax.broadcasted_iota(jnp.int32, live_ref.shape, 0) < live_count, 1.0, 0.0
    )
    entries = table_ref.shape[0]
    history = entries // owner_ref.shape[0]
    piece_tokens = pages_dev * page_tokens
    for numbers, bias_ref in zip(stages, bias_refs):
        token = lax.broadcasted_iota(jnp.int32, bias_ref.shape, 1)
        page = jnp.full(bias_ref.shape, -1, jnp.int32)
        for i, number in enumerate(numbers):
            local = lax.shift_right_logical(
                token - i * piece_tokens, page_tokens.bit_length() - 1
            )
            page = jnp.where(token >= i * piece_tokens, (me ^ number) * pages_dev + local, page)
        masked = token >= len(numbers) * piece_tokens
        for e in range(entries):
            other = jnp.where(e // history == branch, -1, table_ref[e])
            masked = masked | (page == other)
        bias_ref[...] = jnp.where(masked, MASKED, 0.0)
    for copy in copies[3:]:
        copy.wait()


def prepare(queries, shard, span_lengths, owner_branch, branch_table, stages):
    vmem = pl.BlockSpec(memory_space=pltpu.VMEM)
    tables = (span_lengths, owner_branch, branch_table.reshape(-1))
    inputs = [
        pltpu.with_memory_space_constraint(value, pltpu.HBM) for value in (queries, shard) + tables
    ]
    shapes = [
        jax.ShapeDtypeStruct(queries.shape, queries.dtype),
        jax.ShapeDtypeStruct(shard.shape, shard.dtype),
        jax.ShapeDtypeStruct((queries.shape[0], HD), jnp.float32),
    ]
    for numbers in stages:
        held = len(numbers) * shard.shape[0] * shard.shape[1]
        shapes.append(jax.ShapeDtypeStruct((1, held + -held % HD), jnp.float32))
    return pl.pallas_call(
        functools.partial(prepare_kernel, stages=stages),
        out_shape=shapes,
        in_specs=[pl.BlockSpec(memory_space=pltpu.HBM)] * len(inputs),
        out_specs=[vmem] * len(shapes),
        scratch_shapes=[pltpu.SMEM(table.shape, table.dtype) for table in tables]
        + [pltpu.SemaphoreType.DMA((len(inputs),))],
        compiler_params=pltpu.CompilerParams(vmem_limit_bytes=4 << 20),
        name="prepare",
    )(*inputs)


def attention_kernel(*refs, count, first, last):
    q_ref, bias_ref, live_ref = refs[:3]
    piece_refs = refs[3 : 3 + count]
    rest = list(refs[3 + count :])
    old_sums, old_max = (None, None) if first else (rest.pop(0), rest.pop(0))
    out_ref, out_max = (rest.pop(0), None) if last else (rest.pop(0), rest.pop(0))
    keys, values = rest
    rows = q_ref.shape[0]
    tokens = keys.shape[1]
    piece_tokens = piece_refs[0].shape[0] * piece_refs[0].shape[1]
    values[:, :, HD:] = jnp.ones((KVH, tokens, HD), jnp.bfloat16)
    held = count * piece_tokens
    if held < tokens:
        keys[:, held:, :] = jnp.zeros((KVH, tokens - held, HD), jnp.bfloat16)
        values[:, held:, :HD] = jnp.zeros((KVH, tokens - held, HD), jnp.bfloat16)
    for i in range(count):
        block = piece_refs[i][...].reshape(piece_tokens, 2 * KVH * HD)
        span = slice(i * piece_tokens, (i + 1) * piece_tokens)
        for h in range(KVH):
            keys[h, span, :] = block[:, h * HD : (h + 1) * HD]
            values[h, span, :HD] = block[:, (KVH + h) * HD : (KVH + h + 1) * HD]
    bias = bias_ref[...]
    live = live_ref[...] > 0.0
    for q_head in range(QH):
        h = q_head // GROUP
        lanes = slice(q_head * HD, (q_head + 1) * HD)
        wide = slice(q_head * 2 * HD, (q_head + 1) * 2 * HD)
        scores = lax.dot_general(
            q_ref[:, lanes], keys[h], (((1,), (1,)), ((), ())), preferred_element_type=jnp.float32
        )
        scores = scores + bias
        row_max = jnp.broadcast_to(jnp.max(scores, -1, keepdims=True), (rows, HD))
        if not first:
            before = old_max[:, lanes]
            row_max = jnp.maximum(row_max, before)
        weights = jnp.concatenate(
            [
                jnp.exp2((scores[:, t : t + HD] - row_max) * EXP2_SCALE).astype(jnp.bfloat16)
                for t in range(0, tokens, HD)
            ],
            1,
        )
        sums = jnp.dot(weights, values[h], preferred_element_type=jnp.float32)
        mixed, totals = sums[:, :HD], sums[:, HD:]
        if not first:
            factor = jnp.exp2((before - row_max) * EXP2_SCALE)
            old = old_sums[:, wide]
            mixed, totals = mixed + old[:, :HD] * factor, totals + old[:, HD:] * factor
        if last:
            out_ref[:, lanes] = jnp.where(live, mixed / totals, 0.0).astype(jnp.bfloat16)
        else:
            out_ref[:, wide] = jnp.concatenate([mixed, totals], 1)
            out_max[:, lanes] = row_max


def attend_pieces(queries, bias, live, pieces, state, last):
    rows, features = queries.shape
    count = len(pieces)
    tokens = bias.shape[1]
    vmem = pl.BlockSpec(memory_space=pltpu.VMEM)
    state_shape = (
        jax.ShapeDtypeStruct((rows, 2 * features), jnp.float32),
        jax.ShapeDtypeStruct((rows, features), jnp.float32),
    )
    return pl.pallas_call(
        functools.partial(attention_kernel, count=count, first=not state, last=last),
        out_shape=jax.ShapeDtypeStruct((rows, features), jnp.bfloat16) if last else state_shape,
        in_specs=[vmem] * (3 + count + len(state)),
        out_specs=vmem if last else (vmem, vmem),
        scratch_shapes=[
            pltpu.VMEM((KVH, tokens, HD), jnp.bfloat16),
            pltpu.VMEM((KVH, tokens, 2 * HD), jnp.bfloat16),
        ],
        compiler_params=pltpu.CompilerParams(vmem_limit_bytes=32 << 20),
        cost_estimate=pl.CostEstimate(
            flops=4 * rows * features * tokens,
            bytes_accessed=4 * rows * features + 2 * tokens * KVH * HD * 2,
            transcendentals=rows * QH * tokens,
        ),
        name="attention_last" if last else "attention_stage",
    )(queries, bias, live, *pieces, *state)


def attend_staged(queries, kv_pool, span_lengths, owner_branch, branch_table):
    stages = [step[1] for step in PLAN if step[0] == "attend"]
    held = {0: kv_pool}
    marks = {}
    state, stage, biases = (), 0, None
    for step in PLAN:
        earlier = [marks[name] for name in step[-1]]
        if step[0] == "prepare":
            queries, own, live, *biases = prepare(
                after(queries, *earlier), kv_pool, span_lengths, owner_branch, branch_table, stages
            )
            marks["prepare"] = live
        elif step[0] == "attend":
            pieces = [own if number == 0 else held[number] for number in step[1]]
            bias = after(biases[stage], *earlier)
            stage += 1
            state = attend_pieces(queries, bias, live, pieces, state, stage == len(stages))
            if stage < len(stages):
                marks["attend%d" % stage] = state[1]
        else:
            number = step[1] ^ MOVES[step[0]]
            held[number] = permute(after(held[step[1]], *earlier), step[0])
            marks[number] = held[number]
    return state


def attend_anywhere(queries, kv_pool, span_lengths, owner_branch, prefix_table, branch_table):
    device_count = lax.axis_size("seq")
    self_index = lax.axis_index("seq")
    owner_width = device_count // span_lengths.shape[0]
    branch = owner_branch[self_index // owner_width]
    live_count = span_lengths[branch] - self_index % owner_width * queries.shape[0]
    slot_branch = page_owners(prefix_table, branch_table, kv_pool.shape[0] * device_count)
    page_allowed = (slot_branch < 0) | (slot_branch == branch)
    return attend_general(queries, kv_pool, page_allowed, live_count)


def per_device(queries, kv_pool, span_lengths, owner_branch, prefix_table, branch_table):
    if lax.axis_size("seq") == GATHER_DEVICES and kv_pool.shape[1] == 8:
        return attend_staged(queries, kv_pool, span_lengths, owner_branch, branch_table)
    return attend_anywhere(
        queries, kv_pool, span_lengths, owner_branch, prefix_table, branch_table
    )


def solution(mesh):
    return jax.shard_map(
        per_device,
        mesh=mesh,
        in_specs=(
            P(("grp", "seq"), None),
            P(("grp", "seq"), None, None),
            P("grp"),
            P("grp"),
            P("grp"),
            P("grp", None),
        ),
        out_specs=P(("grp", "seq"), None),
        check_vma=False,
    )
```

```python
import functools
import math

import jax
import jax.numpy as jnp
from jax import lax
from jax.experimental import pallas as pl
from jax.experimental.pallas import tpu as pltpu
from jax.sharding import PartitionSpec as P

QH = 32
KVH = 4
HD = 128
GROUP = QH // KVH
EXP2_SCALE = math.log2(math.e) / math.sqrt(HD)
GATHER_DEVICES = 16
TOGETHER = 4
MASKED = -1e30


def page_owners(prefix_table, branch_table, pool_size):
    page_ids = jnp.arange(pool_size, dtype=jnp.int32)
    is_prefix = jnp.any(prefix_table[:, None] == page_ids[None, :], 0)
    flat_table = branch_table.reshape(-1)
    table_branch = jnp.arange(flat_table.shape[0], dtype=jnp.int32) // branch_table.shape[1]
    owner_of = jnp.sum(
        jnp.where(flat_table[:, None] == page_ids[None, :], table_branch[:, None], 0), 0
    )
    return jnp.where(is_prefix, -1, owner_of)


def absorb(carry, query_heads, pages, block_allowed):
    run_max, run_total, run_acc = carry
    page_tokens = pages.shape[1]
    token_count = pages.shape[0] * page_tokens
    kv_tokens = pages.reshape(token_count, 2, KVH, HD)
    keys = kv_tokens[:, 0]
    values = kv_tokens[:, 1]
    scores = jnp.einsum("rkgd,tkd->rkgt", query_heads, keys, preferred_element_type=jnp.float32) * (
        1.0 / math.sqrt(HD)
    )
    allowed = jnp.repeat(block_allowed, page_tokens)[None, None, None, :]
    masked = jnp.where(allowed, scores, -1e30)
    new_max = jnp.maximum(run_max, jnp.max(masked, -1))
    weights = jnp.where(allowed, jnp.exp(scores - new_max[..., None]), 0.0).astype(jnp.bfloat16)
    factor = jnp.exp(run_max - new_max)
    new_total = run_total * factor + jnp.sum(weights.astype(jnp.float32), -1)
    new_acc = run_acc * factor[..., None] + jnp.einsum(
        "rkgt,tkd->rkgd", weights, values, preferred_element_type=jnp.float32
    )
    return (new_max, new_total, new_acc)


def attend_general(queries, kv_pool, page_allowed, live_count):
    row_count = queries.shape[0]
    pages = lax.all_gather(kv_pool, "seq", axis=0, tiled=True)
    page_tokens = pages.shape[1]
    block_pages = max(1, max(128, 32768 // row_count) // page_tokens)
    while pages.shape[0] % block_pages:
        block_pages = block_pages - 1
    blocks = pages.reshape((-1, block_pages) + pages.shape[1:])
    block_allowed = page_allowed.reshape(-1, block_pages)
    query_heads = queries.reshape(row_count, KVH, GROUP, HD)
    start = (
        jnp.full((row_count, KVH, GROUP), -1e30, jnp.float32),
        jnp.zeros((row_count, KVH, GROUP), jnp.float32),
        jnp.zeros((row_count, KVH, GROUP, HD), jnp.float32),
    )

    def scan_step(state, inputs):
        block, allowed = inputs
        return (absorb(state, query_heads, block, allowed), None)

    (run_max, run_total, run_acc), unused = lax.scan(scan_step, start, (blocks, block_allowed))
    mixed = (run_acc / run_total[..., None]).reshape(row_count, QH * HD)
    live = jnp.arange(row_count, dtype=jnp.int32) < live_count
    return jnp.where(live[:, None], mixed, 0.0).astype(jnp.bfloat16)


MOVES = {"core": 1, "x": 2, "z1": 4, "z2": 8}
PLAN = (
    ("z2", 0, ()),
    ("z1", 0, ()),
    ("x", 0, ()),
    ("core", 0, ()),
    ("prepare", ()),
    ("x", 4, ("prepare",)),
    ("z1", 8, ()),
    ("x", 8, ()),
    ("x", 12, ()),
    ("core", 2, ()),
    ("core", 4, ()),
    ("core", 6, ()),
    ("core", 8, ()),
    ("core", 10, ()),
    ("core", 12, ()),
    ("attend", (0, 1, 2, 3, 4, 5, 6, 7), ()),
    ("core", 14, ("attend1",)),
    ("attend", (8, 9, 10, 11, 12, 13, 14, 15), ()),
)


def permute(block, move):
    pairs = [(index, index ^ MOVES[move]) for index in range(GATHER_DEVICES)]
    return lax.ppermute(block, "seq", pairs)


def after(value, *earlier):
    return lax.optimization_barrier((value,) + earlier)[0] if earlier else value


def prepare_kernel(
    q_ref, shard_ref, lengths_in, owner_in, table_in, q_out, shard_out, live_ref, keep_ref, bias_ref, *rest
):
    lengths_ref, owner_ref, table_ref, sems = rest
    ends = (
        (lengths_in, lengths_ref),
        (owner_in, owner_ref),
        (table_in, table_ref),
        (q_ref, q_out),
        (shard_ref, shard_out),
    )
    copies = [pltpu.make_async_copy(*pair, sems.at[i]) for i, pair in enumerate(ends)]
    for copy in copies:
        copy.start()
    keep_ref[...] = jnp.ones(keep_ref.shape, jnp.float32)
    for copy in copies[:3]:
        copy.wait()
    pages_dev, page_tokens = shard_ref.shape[:2]
    piece_tokens = pages_dev * page_tokens
    me = lax.axis_index("seq")
    rows = q_ref.shape[0]
    owner_width = GATHER_DEVICES // owner_ref.shape[0]
    branch = owner_ref[me // owner_width]
    live_count = lengths_ref[branch] - me % owner_width * rows
    live_ref[...] = jnp.where(
        lax.broadcasted_iota(jnp.int32, live_ref.shape, 0) < live_count, 1.0, 0.0
    )
    entries = table_ref.shape[0]
    history = entries // owner_ref.shape[0]
    token = lax.broadcasted_iota(jnp.int32, bias_ref.shape, 1)
    bias = jnp.zeros(bias_ref.shape, jnp.float32)
    for e in range(entries):
        page = table_ref[e]
        device = page // pages_dev
        begin = (device ^ me) * piece_tokens + (page - device * pages_dev) * page_tokens
        seen = jnp.where(branch == e // history, 1.0, 0.0)
        rows_of_page = pl.ds(pl.multiple_of(begin, page_tokens), page_tokens)
        keep_ref[rows_of_page, :] = jnp.full((page_tokens, HD), seen, jnp.float32)
        in_page = (token >= begin) & (token < begin + page_tokens)
        bias = jnp.where(in_page, (1.0 - seen) * MASKED, bias)
    bias_ref[...] = bias
    for copy in copies[3:]:
        copy.wait()


def prepare(queries, shard, span_lengths, owner_branch, branch_table):
    vmem = pl.BlockSpec(memory_space=pltpu.VMEM)
    tables = (span_lengths, owner_branch, branch_table.reshape(-1))
    inputs = [
        pltpu.with_memory_space_constraint(value, pltpu.HBM) for value in (queries, shard) + tables
    ]
    tokens = GATHER_DEVICES * shard.shape[0] * shard.shape[1]
    shapes = [
        jax.ShapeDtypeStruct(queries.shape, queries.dtype),
        jax.ShapeDtypeStruct(shard.shape, shard.dtype),
        jax.ShapeDtypeStruct((queries.shape[0], HD), jnp.float32),
        jax.ShapeDtypeStruct((tokens, HD), jnp.float32),
        jax.ShapeDtypeStruct((1, tokens), jnp.float32),
    ]
    return pl.pallas_call(
        prepare_kernel,
        out_shape=shapes,
        in_specs=[pl.BlockSpec(memory_space=pltpu.HBM)] * len(inputs),
        out_specs=[vmem] * len(shapes),
        scratch_shapes=[pltpu.SMEM(table.shape, table.dtype) for table in tables]
        + [pltpu.SemaphoreType.DMA((len(inputs),))],
        compiler_params=pltpu.CompilerParams(vmem_limit_bytes=4 << 20),
        name="prepare",
    )(*inputs)


def lay_out(piece_ref, h, keep):
    piece_tokens = piece_ref.shape[0] * piece_ref.shape[1]
    keys = piece_ref[:, :, h * HD : (h + 1) * HD].reshape(piece_tokens, HD)
    values = piece_ref[:, :, (KVH + h) * HD : (KVH + h + 1) * HD].reshape(piece_tokens, HD)
    return keys, values * keep, keep


def stage_sums(q_ref, keep_ref, piece_refs, numbers, keys, values, old_sums, give):
    tokens = keys.shape[1]
    piece_tokens = piece_refs[0].shape[0] * piece_refs[0].shape[1]
    held = len(numbers) * piece_tokens
    if held < tokens:
        keys[:, held:, :] = jnp.zeros((KVH, tokens - held, HD), jnp.bfloat16)
        values[:, held:, :] = jnp.zeros((KVH, tokens - held, 2 * HD), jnp.bfloat16)
    for i, number in enumerate(numbers):
        keep = keep_ref[number * piece_tokens : (number + 1) * piece_tokens, :].astype(jnp.bfloat16)
        span = slice(i * piece_tokens, (i + 1) * piece_tokens)
        for h in range(KVH):
            keys[h, span, :], values[h, span, :HD], values[h, span, HD:] = lay_out(
                piece_refs[i], h, keep
            )
    rows = q_ref.shape[0]
    for begin in range(0, QH, TOGETHER):
        h = begin // GROUP
        heads = range(begin, begin + TOGETHER)
        q = jnp.concatenate([q_ref[:, n * HD : (n + 1) * HD] for n in heads], 0)
        scores = lax.dot_general(
            q, keys[h], (((1,), (1,)), ((), ())), preferred_element_type=jnp.float32
        )
        weights = jnp.exp2(scores * EXP2_SCALE).astype(jnp.bfloat16)
        sums = jnp.dot(weights, values[h], preferred_element_type=jnp.float32)
        for i, n in enumerate(heads):
            part = sums[i * rows : (i + 1) * rows]
            if old_sums is not None:
                part = part + old_sums[:, n * 2 * HD : (n + 1) * 2 * HD]
            give(n, part)


def stage_kernel(*refs, numbers, first):
    q_ref, keep_ref = refs[:2]
    piece_refs = refs[2 : 2 + len(numbers)]
    rest = list(refs[2 + len(numbers) :])
    old_sums = None if first else rest.pop(0)
    out_ref, keys, values = rest

    def give(n, part):
        out_ref[:, n * 2 * HD : (n + 1) * 2 * HD] = part

    stage_sums(q_ref, keep_ref, piece_refs, numbers, keys, values, old_sums, give)


def last_kernel(*refs, numbers):
    q_ref, keep_ref, live_ref, bias_ref = refs[:4]
    piece_refs = refs[4 : 4 + GATHER_DEVICES]
    old_sums, out_ref, keys, values, out_vmem, all_keys, all_values, sems = refs[4 + GATHER_DEVICES :]
    rows = q_ref.shape[0]
    live = live_ref[...] > 0.0
    chunk = GROUP * HD
    copies = [
        pltpu.make_async_copy(
            out_vmem.at[:, h * chunk : (h + 1) * chunk],
            out_ref.at[:, h * chunk : (h + 1) * chunk],
            sems.at[h],
        )
        for h in range(KVH)
    ]
    added = [jnp.zeros((rows, HD), jnp.float32), jnp.full((rows, HD), 1.0, jnp.float32)]

    def give(n, part):
        mixed, totals = part[:, :HD], part[:, HD:]
        added[0] = added[0] + totals
        added[1] = jnp.minimum(added[1], totals)
        inverse = pl.reciprocal(totals, approx=True)
        inverse = inverse * (2.0 - totals * inverse)
        lanes = slice(n * HD, (n + 1) * HD)
        out_vmem[:, lanes] = jnp.where(live, mixed * inverse, 0.0).astype(jnp.bfloat16)
        if n % GROUP == GROUP - 1:
            copies[n // GROUP].start()

    new_refs = [piece_refs[number] for number in numbers]
    stage_sums(q_ref, keep_ref, new_refs, numbers, keys, values, old_sums, give)
    fits = (added[0] <= 2.0**100) & (added[1] >= 2.0**-100)
    fits = jnp.min(jnp.where(fits, 1.0, 0.0).reshape(rows // 8, 8, HD), 0)
    fits = jnp.min(fits)
    for copy in copies:
        copy.wait()

    @pl.when(fits < 0.5)
    def with_row_maxima():
        bias = bias_ref[...]
        piece_tokens = piece_refs[0].shape[0] * piece_refs[0].shape[1]
        for h in range(KVH):
            for number in range(GATHER_DEVICES):
                span = slice(number * piece_tokens, (number + 1) * piece_tokens)
                keep = keep_ref[span, :].astype(jnp.bfloat16)
                all_keys[span, :], all_values[span, :HD], all_values[span, HD:] = lay_out(
                    piece_refs[number], h, keep
                )

            def one_head(g, unused):
                lanes = pl.ds(pl.multiple_of((h * GROUP + g) * HD, HD), HD)
                scores = lax.dot_general(
                    q_ref[:, lanes],
                    all_keys[...],
                    (((1,), (1,)), ((), ())),
                    preferred_element_type=jnp.float32,
                )
                scores = scores + bias
                row_max = jnp.max(scores, -1, keepdims=True)
                weights = jnp.exp2((scores - row_max) * EXP2_SCALE).astype(jnp.bfloat16)
                sums = jnp.dot(weights, all_values[...], preferred_element_type=jnp.float32)
                mixed = jnp.where(live, sums[:, :HD] / sums[:, HD:], 0.0)
                out_vmem[:, lanes] = mixed.astype(jnp.bfloat16)
                return unused

            lax.fori_loop(0, GROUP, one_head, 0)
        for copy in copies:
            copy.start()
        for copy in copies:
            copy.wait()


def attend_pieces(queries, keep, live, bias, pieces, numbers, state, last):
    rows, features = queries.shape
    piece_tokens = pieces[numbers[0]].shape[0] * pieces[numbers[0]].shape[1]
    held = len(numbers) * piece_tokens
    tokens = held + -held % HD
    vmem = pl.BlockSpec(memory_space=pltpu.VMEM)
    scratch = [
        pltpu.VMEM((KVH, tokens, HD), jnp.bfloat16),
        pltpu.VMEM((KVH, tokens, 2 * HD), jnp.bfloat16),
    ]
    if last:
        everything = GATHER_DEVICES * piece_tokens
        scratch += [
            pltpu.VMEM((rows, features), jnp.bfloat16),
            pltpu.VMEM((everything, HD), jnp.bfloat16),
            pltpu.VMEM((everything, 2 * HD), jnp.bfloat16),
            pltpu.SemaphoreType.DMA((KVH,)),
        ]
        kernel = functools.partial(last_kernel, numbers=numbers)
        operands = [queries, keep, live, bias] + [pieces[n] for n in range(GATHER_DEVICES)]
        out_shape = jax.ShapeDtypeStruct((rows, features), jnp.bfloat16)
    else:
        kernel = functools.partial(stage_kernel, numbers=numbers, first=not state)
        operands = [queries, keep] + [pieces[n] for n in numbers]
        out_shape = jax.ShapeDtypeStruct((rows, 2 * features), jnp.float32)
    operands += state
    return pl.pallas_call(
        kernel,
        out_shape=out_shape,
        in_specs=[vmem] * len(operands),
        out_specs=pl.BlockSpec(memory_space=pltpu.HBM) if last else vmem,
        scratch_shapes=scratch,
        compiler_params=pltpu.CompilerParams(vmem_limit_bytes=24 << 20),
        cost_estimate=pl.CostEstimate(
            flops=4 * rows * features * tokens,
            bytes_accessed=4 * rows * features + 2 * tokens * KVH * HD * 2,
            transcendentals=rows * QH * tokens,
        ),
        name="attention_last" if last else "attention_stage",
    )(*operands)


def attend_staged(queries, kv_pool, span_lengths, owner_branch, branch_table):
    held = {0: kv_pool}
    marks = {}
    state, stage, stages = [], 0, sum(step[0] == "attend" for step in PLAN)
    for step in PLAN:
        earlier = [marks[name] for name in step[-1]]
        if step[0] == "prepare":
            queries, own, live, keep, bias = prepare(
                after(queries, *earlier), kv_pool, span_lengths, owner_branch, branch_table
            )
            marks["prepare"] = live
        elif step[0] == "attend":
            stage += 1
            pieces = held | {0: own}
            state = [
                attend_pieces(
                    queries, after(keep, *earlier), live, bias, pieces, step[1], state, stage == stages
                )
            ]
            if stage < stages:
                marks["attend%d" % stage] = state[0]
        else:
            number = step[1] ^ MOVES[step[0]]
            held[number] = permute(after(held[step[1]], *earlier), step[0])
            marks[number] = held[number]
    return state[0]


def attend_anywhere(queries, kv_pool, span_lengths, owner_branch, prefix_table, branch_table):
    device_count = lax.axis_size("seq")
    self_index = lax.axis_index("seq")
    owner_width = device_count // span_lengths.shape[0]
    branch = owner_branch[self_index // owner_width]
    live_count = span_lengths[branch] - self_index % owner_width * queries.shape[0]
    slot_branch = page_owners(prefix_table, branch_table, kv_pool.shape[0] * device_count)
    page_allowed = (slot_branch < 0) | (slot_branch == branch)
    return attend_general(queries, kv_pool, page_allowed, live_count)


def per_device(queries, kv_pool, span_lengths, owner_branch, prefix_table, branch_table):
    if lax.axis_size("seq") == GATHER_DEVICES and kv_pool.shape[1] == 8:
        return attend_staged(queries, kv_pool, span_lengths, owner_branch, branch_table)
    return attend_anywhere(
        queries, kv_pool, span_lengths, owner_branch, prefix_table, branch_table
    )


def solution(mesh):
    return jax.shard_map(
        per_device,
        mesh=mesh,
        in_specs=(
            P(("grp", "seq"), None),
            P(("grp", "seq"), None, None),
            P("grp"),
            P("grp"),
            P("grp"),
            P("grp", None),
        ),
        out_specs=P(("grp", "seq"), None),
        check_vma=False,
    )
```

```python
import functools
import math

import jax
import jax.numpy as jnp
from jax import lax
from jax.experimental import pallas as pl
from jax.experimental.pallas import tpu as pltpu
from jax.sharding import PartitionSpec as P

QH = 32
KVH = 4
HD = 128
GROUP = QH // KVH
EXP2_SCALE = math.log2(math.e) / math.sqrt(HD)
GATHER_DEVICES = 16
TOGETHER = 2
MASKED = -1e30


def page_owners(prefix_table, branch_table, pool_size):
    page_ids = jnp.arange(pool_size, dtype=jnp.int32)
    is_prefix = jnp.any(prefix_table[:, None] == page_ids[None, :], 0)
    flat_table = branch_table.reshape(-1)
    table_branch = jnp.arange(flat_table.shape[0], dtype=jnp.int32) // branch_table.shape[1]
    owner_of = jnp.sum(
        jnp.where(flat_table[:, None] == page_ids[None, :], table_branch[:, None], 0), 0
    )
    return jnp.where(is_prefix, -1, owner_of)


def absorb(carry, query_heads, pages, block_allowed):
    run_max, run_total, run_acc = carry
    page_tokens = pages.shape[1]
    token_count = pages.shape[0] * page_tokens
    kv_tokens = pages.reshape(token_count, 2, KVH, HD)
    keys = kv_tokens[:, 0]
    values = kv_tokens[:, 1]
    scores = jnp.einsum("rkgd,tkd->rkgt", query_heads, keys, preferred_element_type=jnp.float32) * (
        1.0 / math.sqrt(HD)
    )
    allowed = jnp.repeat(block_allowed, page_tokens)[None, None, None, :]
    masked = jnp.where(allowed, scores, -1e30)
    new_max = jnp.maximum(run_max, jnp.max(masked, -1))
    weights = jnp.where(allowed, jnp.exp(scores - new_max[..., None]), 0.0).astype(jnp.bfloat16)
    factor = jnp.exp(run_max - new_max)
    new_total = run_total * factor + jnp.sum(weights.astype(jnp.float32), -1)
    new_acc = run_acc * factor[..., None] + jnp.einsum(
        "rkgt,tkd->rkgd", weights, values, preferred_element_type=jnp.float32
    )
    return (new_max, new_total, new_acc)


def attend_general(queries, kv_pool, page_allowed, live_count):
    row_count = queries.shape[0]
    pages = lax.all_gather(kv_pool, "seq", axis=0, tiled=True)
    page_tokens = pages.shape[1]
    block_pages = max(1, max(128, 32768 // row_count) // page_tokens)
    while pages.shape[0] % block_pages:
        block_pages = block_pages - 1
    blocks = pages.reshape((-1, block_pages) + pages.shape[1:])
    block_allowed = page_allowed.reshape(-1, block_pages)
    query_heads = queries.reshape(row_count, KVH, GROUP, HD)
    start = (
        jnp.full((row_count, KVH, GROUP), -1e30, jnp.float32),
        jnp.zeros((row_count, KVH, GROUP), jnp.float32),
        jnp.zeros((row_count, KVH, GROUP, HD), jnp.float32),
    )

    def scan_step(state, inputs):
        block, allowed = inputs
        return (absorb(state, query_heads, block, allowed), None)

    (run_max, run_total, run_acc), unused = lax.scan(scan_step, start, (blocks, block_allowed))
    mixed = (run_acc / run_total[..., None]).reshape(row_count, QH * HD)
    live = jnp.arange(row_count, dtype=jnp.int32) < live_count
    return jnp.where(live[:, None], mixed, 0.0).astype(jnp.bfloat16)


MOVES = {"core": 1, "x": 2, "z1": 4, "z2": 8}
PLAN = (
    ("z2", 0, ()),
    ("z1", 0, ()),
    ("x", 0, ()),
    ("core", 0, ()),
    ("prepare", ()),
    ("x", 4, ("prepare",)),
    ("z1", 8, ()),
    ("x", 8, ()),
    ("x", 12, ()),
    ("core", 2, ()),
    ("core", 4, ()),
    ("core", 6, ()),
    ("core", 8, ()),
    ("core", 10, ()),
    ("core", 12, ()),
    ("attend", (0, 1, 2, 3, 4, 5, 6, 7, 8), ()),
    ("core", 14, ("attend1",)),
    ("attend", (9, 10, 11, 12, 13, 14, 15), ()),
)


def permute(block, move):
    pairs = [(index, index ^ MOVES[move]) for index in range(GATHER_DEVICES)]
    return lax.ppermute(block, "seq", pairs)


def after(value, *earlier):
    return lax.optimization_barrier((value,) + earlier)[0] if earlier else value


def prepare_kernel(
    q_ref, shard_ref, lengths_in, owner_in, table_in, q_out, shard_out, live_ref, keep_ref, bias_ref, *rest
):
    lengths_ref, owner_ref, table_ref, sems = rest
    ends = (
        (lengths_in, lengths_ref),
        (owner_in, owner_ref),
        (table_in, table_ref),
        (q_ref, q_out),
        (shard_ref, shard_out),
    )
    copies = [pltpu.make_async_copy(*pair, sems.at[i]) for i, pair in enumerate(ends)]
    for copy in copies:
        copy.start()
    keep_ref[...] = jnp.ones(keep_ref.shape, jnp.float32)
    for copy in copies[:3]:
        copy.wait()
    pages_dev, page_tokens = shard_ref.shape[:2]
    piece_tokens = pages_dev * page_tokens
    me = lax.axis_index("seq")
    rows = q_ref.shape[0]
    owner_width = GATHER_DEVICES // owner_ref.shape[0]
    branch = owner_ref[me // owner_width]
    live_count = lengths_ref[branch] - me % owner_width * rows
    live_ref[...] = jnp.where(
        lax.broadcasted_iota(jnp.int32, live_ref.shape, 0) < live_count, 1.0, 0.0
    )
    entries = table_ref.shape[0]
    history = entries // owner_ref.shape[0]
    token = lax.broadcasted_iota(jnp.int32, bias_ref.shape, 1)
    bias = jnp.zeros(bias_ref.shape, jnp.float32)
    for e in range(entries):
        page = table_ref[e]
        device = page // pages_dev
        begin = (device ^ me) * piece_tokens + (page - device * pages_dev) * page_tokens
        seen = jnp.where(branch == e // history, 1.0, 0.0)
        rows_of_page = pl.ds(pl.multiple_of(begin, page_tokens), page_tokens)
        keep_ref[rows_of_page, :] = jnp.full((page_tokens, HD), seen, jnp.float32)
        in_page = (token >= begin) & (token < begin + page_tokens)
        bias = jnp.where(in_page, (1.0 - seen) * MASKED, bias)
    bias_ref[...] = bias
    for copy in copies[3:]:
        copy.wait()


def prepare(queries, shard, span_lengths, owner_branch, branch_table):
    vmem = pl.BlockSpec(memory_space=pltpu.VMEM)
    tables = (span_lengths, owner_branch, branch_table.reshape(-1))
    inputs = [
        pltpu.with_memory_space_constraint(value, pltpu.HBM) for value in (queries, shard) + tables
    ]
    tokens = GATHER_DEVICES * shard.shape[0] * shard.shape[1]
    shapes = [
        jax.ShapeDtypeStruct(queries.shape, queries.dtype),
        jax.ShapeDtypeStruct(shard.shape, shard.dtype),
        jax.ShapeDtypeStruct((queries.shape[0], HD), jnp.float32),
        jax.ShapeDtypeStruct((tokens, HD), jnp.float32),
        jax.ShapeDtypeStruct((1, tokens), jnp.float32),
    ]
    return pl.pallas_call(
        prepare_kernel,
        out_shape=shapes,
        in_specs=[pl.BlockSpec(memory_space=pltpu.HBM)] * len(inputs),
        out_specs=[vmem] * len(shapes),
        scratch_shapes=[pltpu.SMEM(table.shape, table.dtype) for table in tables]
        + [pltpu.SemaphoreType.DMA((len(inputs),))],
        compiler_params=pltpu.CompilerParams(vmem_limit_bytes=4 << 20),
        name="prepare",
    )(*inputs)


def lay_out(piece_ref, h, keep):
    piece_tokens = piece_ref.shape[0] * piece_ref.shape[1]
    keys = piece_ref[:, :, h * HD : (h + 1) * HD].reshape(piece_tokens, HD)
    values = piece_ref[:, :, (KVH + h) * HD : (KVH + h + 1) * HD].reshape(piece_tokens, HD)
    return keys, values * keep, keep


def stage_sums(q_ref, keep_ref, piece_refs, numbers, keys, values, old_sums, give):
    tokens = keys.shape[1]
    piece_tokens = piece_refs[0].shape[0] * piece_refs[0].shape[1]
    held = len(numbers) * piece_tokens
    if held < tokens:
        keys[:, held:, :] = jnp.zeros((KVH, tokens - held, HD), jnp.bfloat16)
        values[:, held:, :] = jnp.zeros((KVH, tokens - held, 2 * HD), jnp.bfloat16)
    for i, number in enumerate(numbers):
        keep = keep_ref[number * piece_tokens : (number + 1) * piece_tokens, :].astype(jnp.bfloat16)
        span = slice(i * piece_tokens, (i + 1) * piece_tokens)
        for h in range(KVH):
            keys[h, span, :], values[h, span, :HD], values[h, span, HD:] = lay_out(
                piece_refs[i], h, keep
            )
    rows = q_ref.shape[0]
    for begin in range(0, QH, TOGETHER):
        h = begin // GROUP
        heads = range(begin, begin + TOGETHER)
        q = jnp.concatenate([q_ref[:, n * HD : (n + 1) * HD] for n in heads], 0)
        scores = lax.dot_general(
            q, keys[h], (((1,), (1,)), ((), ())), preferred_element_type=jnp.float32
        )
        weights = jnp.exp2(scores * EXP2_SCALE).astype(jnp.bfloat16)
        sums = jnp.dot(weights, values[h], preferred_element_type=jnp.float32)
        for i, n in enumerate(heads):
            part = sums[i * rows : (i + 1) * rows]
            if old_sums is not None:
                part = part + old_sums[:, n * 2 * HD : (n + 1) * 2 * HD]
            give(n, part)


def stage_kernel(*refs, numbers, first):
    q_ref, keep_ref = refs[:2]
    piece_refs = refs[2 : 2 + len(numbers)]
    rest = list(refs[2 + len(numbers) :])
    old_sums = None if first else rest.pop(0)
    out_ref, keys, values = rest

    def give(n, part):
        out_ref[:, n * 2 * HD : (n + 1) * 2 * HD] = part

    stage_sums(q_ref, keep_ref, piece_refs, numbers, keys, values, old_sums, give)


def last_kernel(*refs, numbers):
    q_ref, keep_ref, live_ref, bias_ref = refs[:4]
    piece_refs = refs[4 : 4 + GATHER_DEVICES]
    old_sums, out_ref, keys, values, out_vmem, all_keys, all_values, sems = refs[4 + GATHER_DEVICES :]
    rows = q_ref.shape[0]
    live = live_ref[...] > 0.0
    chunk = GROUP * HD
    copies = [
        pltpu.make_async_copy(
            out_vmem.at[:, h * chunk : (h + 1) * chunk],
            out_ref.at[:, h * chunk : (h + 1) * chunk],
            sems.at[h],
        )
        for h in range(KVH)
    ]
    added = [jnp.zeros((rows, HD), jnp.float32), jnp.full((rows, HD), 1.0, jnp.float32)]

    def give(n, part):
        mixed, totals = part[:, :HD], part[:, HD:]
        added[0] = added[0] + totals
        added[1] = jnp.minimum(added[1], totals)
        inverse = pl.reciprocal(totals, approx=True)
        inverse = inverse * (2.0 - totals * inverse)
        lanes = slice(n * HD, (n + 1) * HD)
        out_vmem[:, lanes] = jnp.where(live, mixed * inverse, 0.0).astype(jnp.bfloat16)
        if n % GROUP == GROUP - 1:
            copies[n // GROUP].start()

    new_refs = [piece_refs[number] for number in numbers]
    stage_sums(q_ref, keep_ref, new_refs, numbers, keys, values, old_sums, give)
    fits = (added[0] <= 2.0**100) & (added[1] >= 2.0**-100)
    fits = jnp.min(jnp.where(fits, 1.0, 0.0).reshape(rows // 8, 8, HD), 0)
    fits = jnp.min(fits)
    for copy in copies:
        copy.wait()

    @pl.when(fits < 0.5)
    def with_row_maxima():
        bias = bias_ref[...]
        piece_tokens = piece_refs[0].shape[0] * piece_refs[0].shape[1]
        for h in range(KVH):
            for number in range(GATHER_DEVICES):
                span = slice(number * piece_tokens, (number + 1) * piece_tokens)
                keep = keep_ref[span, :].astype(jnp.bfloat16)
                all_keys[span, :], all_values[span, :HD], all_values[span, HD:] = lay_out(
                    piece_refs[number], h, keep
                )

            def one_head(g, unused):
                lanes = pl.ds(pl.multiple_of((h * GROUP + g) * HD, HD), HD)
                scores = lax.dot_general(
                    q_ref[:, lanes],
                    all_keys[...],
                    (((1,), (1,)), ((), ())),
                    preferred_element_type=jnp.float32,
                )
                scores = scores + bias
                row_max = jnp.max(scores, -1, keepdims=True)
                weights = jnp.exp2((scores - row_max) * EXP2_SCALE).astype(jnp.bfloat16)
                sums = jnp.dot(weights, all_values[...], preferred_element_type=jnp.float32)
                mixed = jnp.where(live, sums[:, :HD] / sums[:, HD:], 0.0)
                out_vmem[:, lanes] = mixed.astype(jnp.bfloat16)
                return unused

            lax.fori_loop(0, GROUP, one_head, 0)
        for copy in copies:
            copy.start()
        for copy in copies:
            copy.wait()


def attend_pieces(queries, keep, live, bias, pieces, numbers, state, last):
    rows, features = queries.shape
    piece_tokens = pieces[numbers[0]].shape[0] * pieces[numbers[0]].shape[1]
    held = len(numbers) * piece_tokens
    tokens = held + -held % HD
    vmem = pl.BlockSpec(memory_space=pltpu.VMEM)
    scratch = [
        pltpu.VMEM((KVH, tokens, HD), jnp.bfloat16),
        pltpu.VMEM((KVH, tokens, 2 * HD), jnp.bfloat16),
    ]
    if last:
        everything = GATHER_DEVICES * piece_tokens
        scratch += [
            pltpu.VMEM((rows, features), jnp.bfloat16),
            pltpu.VMEM((everything, HD), jnp.bfloat16),
            pltpu.VMEM((everything, 2 * HD), jnp.bfloat16),
            pltpu.SemaphoreType.DMA((KVH,)),
        ]
        kernel = functools.partial(last_kernel, numbers=numbers)
        operands = [queries, keep, live, bias] + [pieces[n] for n in range(GATHER_DEVICES)]
        out_shape = jax.ShapeDtypeStruct((rows, features), jnp.bfloat16)
    else:
        kernel = functools.partial(stage_kernel, numbers=numbers, first=not state)
        operands = [queries, keep] + [pieces[n] for n in numbers]
        out_shape = jax.ShapeDtypeStruct((rows, 2 * features), jnp.float32)
    operands += state
    return pl.pallas_call(
        kernel,
        out_shape=out_shape,
        in_specs=[vmem] * len(operands),
        out_specs=pl.BlockSpec(memory_space=pltpu.HBM) if last else vmem,
        scratch_shapes=scratch,
        compiler_params=pltpu.CompilerParams(vmem_limit_bytes=24 << 20),
        cost_estimate=pl.CostEstimate(flops=0, bytes_accessed=0, transcendentals=0),
        name="attention_last" if last else "attention_stage",
    )(*operands)


def attend_staged(queries, kv_pool, span_lengths, owner_branch, branch_table):
    held = {0: kv_pool}
    marks = {}
    state, stage, stages = [], 0, sum(step[0] == "attend" for step in PLAN)
    for step in PLAN:
        earlier = [marks[name] for name in step[-1]]
        if step[0] == "prepare":
            queries, own, live, keep, bias = prepare(
                after(queries, *earlier), kv_pool, span_lengths, owner_branch, branch_table
            )
            marks["prepare"] = live
        elif step[0] == "attend":
            stage += 1
            pieces = held | {0: own}
            state = [
                attend_pieces(
                    queries, after(keep, *earlier), live, bias, pieces, step[1], state, stage == stages
                )
            ]
            if stage < stages:
                marks["attend%d" % stage] = state[0]
        else:
            number = step[1] ^ MOVES[step[0]]
            held[number] = permute(after(held[step[1]], *earlier), step[0])
            marks[number] = held[number]
    return state[0]


def attend_anywhere(queries, kv_pool, span_lengths, owner_branch, prefix_table, branch_table):
    device_count = lax.axis_size("seq")
    self_index = lax.axis_index("seq")
    owner_width = device_count // span_lengths.shape[0]
    branch = owner_branch[self_index // owner_width]
    live_count = span_lengths[branch] - self_index % owner_width * queries.shape[0]
    slot_branch = page_owners(prefix_table, branch_table, kv_pool.shape[0] * device_count)
    page_allowed = (slot_branch < 0) | (slot_branch == branch)
    return attend_general(queries, kv_pool, page_allowed, live_count)


def per_device(queries, kv_pool, span_lengths, owner_branch, prefix_table, branch_table):
    if lax.axis_size("seq") == GATHER_DEVICES and kv_pool.shape[1] == 8:
        return attend_staged(queries, kv_pool, span_lengths, owner_branch, branch_table)
    return attend_anywhere(
        queries, kv_pool, span_lengths, owner_branch, prefix_table, branch_table
    )


def solution(mesh):
    return jax.shard_map(
        per_device,
        mesh=mesh,
        in_specs=(
            P(("grp", "seq"), None),
            P(("grp", "seq"), None, None),
            P("grp"),
            P("grp"),
            P("grp"),
            P("grp", None),
        ),
        out_specs=P(("grp", "seq"), None),
        check_vma=False,
    )
```

```python
import functools
import math

import jax
import jax.numpy as jnp
from jax import lax
from jax.experimental import pallas as pl
from jax.experimental.pallas import tpu as pltpu
from jax.sharding import PartitionSpec as P

QH = 32
KVH = 4
HD = 128
GROUP = QH // KVH
EXP2_SCALE = math.log2(math.e) / math.sqrt(HD)
GATHER_DEVICES = 16
TOGETHER = 2
MASKED = -1e30


def page_owners(prefix_table, branch_table, pool_size):
    page_ids = jnp.arange(pool_size, dtype=jnp.int32)
    is_prefix = jnp.any(prefix_table[:, None] == page_ids[None, :], 0)
    flat_table = branch_table.reshape(-1)
    table_branch = jnp.arange(flat_table.shape[0], dtype=jnp.int32) // branch_table.shape[1]
    owner_of = jnp.sum(
        jnp.where(flat_table[:, None] == page_ids[None, :], table_branch[:, None], 0), 0
    )
    return jnp.where(is_prefix, -1, owner_of)


def absorb(carry, query_heads, pages, block_allowed):
    run_max, run_total, run_acc = carry
    page_tokens = pages.shape[1]
    token_count = pages.shape[0] * page_tokens
    kv_tokens = pages.reshape(token_count, 2, KVH, HD)
    keys = kv_tokens[:, 0]
    values = kv_tokens[:, 1]
    scores = jnp.einsum("rkgd,tkd->rkgt", query_heads, keys, preferred_element_type=jnp.float32) * (
        1.0 / math.sqrt(HD)
    )
    allowed = jnp.repeat(block_allowed, page_tokens)[None, None, None, :]
    masked = jnp.where(allowed, scores, -1e30)
    new_max = jnp.maximum(run_max, jnp.max(masked, -1))
    weights = jnp.where(allowed, jnp.exp(scores - new_max[..., None]), 0.0).astype(jnp.bfloat16)
    factor = jnp.exp(run_max - new_max)
    new_total = run_total * factor + jnp.sum(weights.astype(jnp.float32), -1)
    new_acc = run_acc * factor[..., None] + jnp.einsum(
        "rkgt,tkd->rkgd", weights, values, preferred_element_type=jnp.float32
    )
    return (new_max, new_total, new_acc)


def attend_general(queries, kv_pool, page_allowed, live_count):
    row_count = queries.shape[0]
    pages = lax.all_gather(kv_pool, "seq", axis=0, tiled=True)
    page_tokens = pages.shape[1]
    block_pages = max(1, max(128, 32768 // row_count) // page_tokens)
    while pages.shape[0] % block_pages:
        block_pages = block_pages - 1
    blocks = pages.reshape((-1, block_pages) + pages.shape[1:])
    block_allowed = page_allowed.reshape(-1, block_pages)
    query_heads = queries.reshape(row_count, KVH, GROUP, HD)
    start = (
        jnp.full((row_count, KVH, GROUP), -1e30, jnp.float32),
        jnp.zeros((row_count, KVH, GROUP), jnp.float32),
        jnp.zeros((row_count, KVH, GROUP, HD), jnp.float32),
    )

    def scan_step(state, inputs):
        block, allowed = inputs
        return (absorb(state, query_heads, block, allowed), None)

    (run_max, run_total, run_acc), unused = lax.scan(scan_step, start, (blocks, block_allowed))
    mixed = (run_acc / run_total[..., None]).reshape(row_count, QH * HD)
    live = jnp.arange(row_count, dtype=jnp.int32) < live_count
    return jnp.where(live[:, None], mixed, 0.0).astype(jnp.bfloat16)


MOVES = {"core": 1, "x": 2, "z1": 4, "z2": 8}
PLAN = (
    ("z2", 0, ()),
    ("z1", 0, ()),
    ("x", 0, ()),
    ("core", 0, ()),
    ("prepare", ()),
    ("x", 4, ("prepare",)),
    ("attend", (0, 4), ()),
    ("z1", 8, ("attend1",)),
    ("x", 8, ()),
    ("x", 12, ()),
    ("core", 2, ()),
    ("core", 4, ()),
    ("core", 6, ()),
    ("core", 8, ()),
    ("core", 10, ()),
    ("core", 12, ()),
    ("attend", (1, 2, 3, 5, 6, 7, 8), ()),
    ("core", 14, ("attend2",)),
    ("attend", (9, 10, 11, 12, 13, 14, 15), ()),
)


def permute(block, move):
    pairs = [(index, index ^ MOVES[move]) for index in range(GATHER_DEVICES)]
    return lax.ppermute(block, "seq", pairs)


def after(value, *earlier):
    return lax.optimization_barrier((value,) + earlier)[0] if earlier else value


def prepare_kernel(
    q_ref, shard_ref, lengths_in, owner_in, table_in, q_out, shard_out, live_ref, keep_ref, bias_ref, *rest
):
    lengths_ref, owner_ref, table_ref, sems = rest
    ends = (
        (lengths_in, lengths_ref),
        (owner_in, owner_ref),
        (table_in, table_ref),
        (q_ref, q_out),
        (shard_ref, shard_out),
    )
    copies = [pltpu.make_async_copy(*pair, sems.at[i]) for i, pair in enumerate(ends)]
    for copy in copies:
        copy.start()
    keep_ref[...] = jnp.ones(keep_ref.shape, jnp.float32)
    for copy in copies[:3]:
        copy.wait()
    pages_dev, page_tokens = shard_ref.shape[:2]
    piece_tokens = pages_dev * page_tokens
    me = lax.axis_index("seq")
    rows = q_ref.shape[0]
    owner_width = GATHER_DEVICES // owner_ref.shape[0]
    branch = owner_ref[me // owner_width]
    live_count = lengths_ref[branch] - me % owner_width * rows
    live_ref[...] = jnp.where(
        lax.broadcasted_iota(jnp.int32, live_ref.shape, 0) < live_count, 1.0, 0.0
    )
    entries = table_ref.shape[0]
    history = entries // owner_ref.shape[0]
    token = lax.broadcasted_iota(jnp.int32, bias_ref.shape, 1)
    bias = jnp.zeros(bias_ref.shape, jnp.float32)
    for e in range(entries):
        page = table_ref[e]
        device = page // pages_dev
        begin = (device ^ me) * piece_tokens + (page - device * pages_dev) * page_tokens
        seen = jnp.where(branch == e // history, 1.0, 0.0)
        rows_of_page = pl.ds(pl.multiple_of(begin, page_tokens), page_tokens)
        keep_ref[rows_of_page, :] = jnp.full((page_tokens, HD), seen, jnp.float32)
        in_page = (token >= begin) & (token < begin + page_tokens)
        bias = jnp.where(in_page, (1.0 - seen) * MASKED, bias)
    bias_ref[...] = bias
    for copy in copies[3:]:
        copy.wait()


def prepare(queries, shard, span_lengths, owner_branch, branch_table):
    vmem = pl.BlockSpec(memory_space=pltpu.VMEM)
    tables = (span_lengths, owner_branch, branch_table.reshape(-1))
    inputs = [
        pltpu.with_memory_space_constraint(value, pltpu.HBM) for value in (queries, shard) + tables
    ]
    tokens = GATHER_DEVICES * shard.shape[0] * shard.shape[1]
    shapes = [
        jax.ShapeDtypeStruct(queries.shape, queries.dtype),
        jax.ShapeDtypeStruct(shard.shape, shard.dtype),
        jax.ShapeDtypeStruct((queries.shape[0], HD), jnp.float32),
        jax.ShapeDtypeStruct((tokens, HD), jnp.float32),
        jax.ShapeDtypeStruct((1, tokens), jnp.float32),
    ]
    return pl.pallas_call(
        prepare_kernel,
        out_shape=shapes,
        in_specs=[pl.BlockSpec(memory_space=pltpu.HBM)] * len(inputs),
        out_specs=[vmem] * len(shapes),
        scratch_shapes=[pltpu.SMEM(table.shape, table.dtype) for table in tables]
        + [pltpu.SemaphoreType.DMA((len(inputs),))],
        compiler_params=pltpu.CompilerParams(vmem_limit_bytes=4 << 20),
        name="prepare",
    )(*inputs)


def lay_out(piece_ref, h, keep):
    piece_tokens = piece_ref.shape[0] * piece_ref.shape[1]
    keys = piece_ref[:, :, h * HD : (h + 1) * HD].reshape(piece_tokens, HD)
    values = piece_ref[:, :, (KVH + h) * HD : (KVH + h + 1) * HD].reshape(piece_tokens, HD)
    return keys, values * keep, keep


def stage_sums(q_ref, keep_ref, piece_refs, numbers, keys, values, old_sums, give):
    tokens = keys.shape[1]
    piece_tokens = piece_refs[0].shape[0] * piece_refs[0].shape[1]
    held = len(numbers) * piece_tokens
    if held < tokens:
        keys[:, held:, :] = jnp.zeros((KVH, tokens - held, HD), jnp.bfloat16)
        values[:, held:, :] = jnp.zeros((KVH, tokens - held, 2 * HD), jnp.bfloat16)
    for i, number in enumerate(numbers):
        keep = keep_ref[number * piece_tokens : (number + 1) * piece_tokens, :].astype(jnp.bfloat16)
        span = slice(i * piece_tokens, (i + 1) * piece_tokens)
        for h in range(KVH):
            keys[h, span, :], values[h, span, :HD], values[h, span, HD:] = lay_out(
                piece_refs[i], h, keep
            )
    rows = q_ref.shape[0]
    for begin in range(0, QH, TOGETHER):
        h = begin // GROUP
        heads = range(begin, begin + TOGETHER)
        q = jnp.concatenate([q_ref[:, n * HD : (n + 1) * HD] for n in heads], 0)
        scores = lax.dot_general(
            q, keys[h], (((1,), (1,)), ((), ())), preferred_element_type=jnp.float32
        )
        weights = jnp.exp2(scores * EXP2_SCALE).astype(jnp.bfloat16)
        sums = jnp.dot(weights, values[h], preferred_element_type=jnp.float32)
        for i, n in enumerate(heads):
            part = sums[i * rows : (i + 1) * rows]
            if old_sums is not None:
                part = part + old_sums[:, n * 2 * HD : (n + 1) * 2 * HD]
            give(n, part)


def stage_kernel(*refs, numbers, first):
    q_ref, keep_ref = refs[:2]
    piece_refs = refs[2 : 2 + len(numbers)]
    rest = list(refs[2 + len(numbers) :])
    old_sums = None if first else rest.pop(0)
    out_ref, keys, values = rest

    def give(n, part):
        out_ref[:, n * 2 * HD : (n + 1) * 2 * HD] = part

    stage_sums(q_ref, keep_ref, piece_refs, numbers, keys, values, old_sums, give)


def last_kernel(*refs, numbers):
    q_ref, keep_ref, live_ref, bias_ref = refs[:4]
    piece_refs = refs[4 : 4 + GATHER_DEVICES]
    old_sums, out_ref, keys, values, out_vmem, all_keys, all_values, sems = refs[4 + GATHER_DEVICES :]
    rows = q_ref.shape[0]
    live = live_ref[...] > 0.0
    chunk = GROUP * HD
    copies = [
        pltpu.make_async_copy(
            out_vmem.at[:, h * chunk : (h + 1) * chunk],
            out_ref.at[:, h * chunk : (h + 1) * chunk],
            sems.at[h],
        )
        for h in range(KVH)
    ]
    added = [jnp.zeros((rows, HD), jnp.float32), jnp.full((rows, HD), 1.0, jnp.float32)]

    def give(n, part):
        mixed, totals = part[:, :HD], part[:, HD:]
        added[0] = added[0] + totals
        added[1] = jnp.minimum(added[1], totals)
        inverse = pl.reciprocal(totals, approx=True)
        inverse = inverse * (2.0 - totals * inverse)
        lanes = slice(n * HD, (n + 1) * HD)
        out_vmem[:, lanes] = jnp.where(live, mixed * inverse, 0.0).astype(jnp.bfloat16)
        if n % GROUP == GROUP - 1:
            copies[n // GROUP].start()

    new_refs = [piece_refs[number] for number in numbers]
    stage_sums(q_ref, keep_ref, new_refs, numbers, keys, values, old_sums, give)
    fits = (added[0] <= 2.0**100) & (added[1] >= 2.0**-100)
    fits = jnp.min(jnp.where(fits, 1.0, 0.0).reshape(rows // 8, 8, HD), 0)
    fits = jnp.min(fits)
    for copy in copies:
        copy.wait()

    @pl.when(fits < 0.5)
    def with_row_maxima():
        bias = bias_ref[...]
        piece_tokens = piece_refs[0].shape[0] * piece_refs[0].shape[1]
        for h in range(KVH):
            for number in range(GATHER_DEVICES):
                span = slice(number * piece_tokens, (number + 1) * piece_tokens)
                keep = keep_ref[span, :].astype(jnp.bfloat16)
                all_keys[span, :], all_values[span, :HD], all_values[span, HD:] = lay_out(
                    piece_refs[number], h, keep
                )

            def one_head(g, unused):
                lanes = pl.ds(pl.multiple_of((h * GROUP + g) * HD, HD), HD)
                scores = lax.dot_general(
                    q_ref[:, lanes],
                    all_keys[...],
                    (((1,), (1,)), ((), ())),
                    preferred_element_type=jnp.float32,
                )
                scores = scores + bias
                row_max = jnp.max(scores, -1, keepdims=True)
                weights = jnp.exp2((scores - row_max) * EXP2_SCALE).astype(jnp.bfloat16)
                sums = jnp.dot(weights, all_values[...], preferred_element_type=jnp.float32)
                mixed = jnp.where(live, sums[:, :HD] / sums[:, HD:], 0.0)
                out_vmem[:, lanes] = mixed.astype(jnp.bfloat16)
                return unused

            lax.fori_loop(0, GROUP, one_head, 0)
        for copy in copies:
            copy.start()
        for copy in copies:
            copy.wait()


def attend_pieces(queries, keep, live, bias, pieces, numbers, state, last):
    rows, features = queries.shape
    piece_tokens = pieces[numbers[0]].shape[0] * pieces[numbers[0]].shape[1]
    held = len(numbers) * piece_tokens
    tokens = held + -held % HD
    vmem = pl.BlockSpec(memory_space=pltpu.VMEM)
    scratch = [
        pltpu.VMEM((KVH, tokens, HD), jnp.bfloat16),
        pltpu.VMEM((KVH, tokens, 2 * HD), jnp.bfloat16),
    ]
    if last:
        everything = GATHER_DEVICES * piece_tokens
        scratch += [
            pltpu.VMEM((rows, features), jnp.bfloat16),
            pltpu.VMEM((everything, HD), jnp.bfloat16),
            pltpu.VMEM((everything, 2 * HD), jnp.bfloat16),
            pltpu.SemaphoreType.DMA((KVH,)),
        ]
        kernel = functools.partial(last_kernel, numbers=numbers)
        operands = [queries, keep, live, bias] + [pieces[n] for n in range(GATHER_DEVICES)]
        out_shape = jax.ShapeDtypeStruct((rows, features), jnp.bfloat16)
    else:
        kernel = functools.partial(stage_kernel, numbers=numbers, first=not state)
        operands = [queries, keep] + [pieces[n] for n in numbers]
        out_shape = jax.ShapeDtypeStruct((rows, 2 * features), jnp.float32)
    operands += state
    return pl.pallas_call(
        kernel,
        out_shape=out_shape,
        in_specs=[vmem] * len(operands),
        out_specs=pl.BlockSpec(memory_space=pltpu.HBM) if last else vmem,
        scratch_shapes=scratch,
        compiler_params=pltpu.CompilerParams(vmem_limit_bytes=24 << 20),
        cost_estimate=pl.CostEstimate(flops=0, bytes_accessed=0, transcendentals=0),
        name="attention_last" if last else "attention_stage",
    )(*operands)


def attend_staged(queries, kv_pool, span_lengths, owner_branch, branch_table):
    held = {0: kv_pool}
    marks = {}
    state, stage, stages = [], 0, sum(step[0] == "attend" for step in PLAN)
    for step in PLAN:
        earlier = [marks[name] for name in step[-1]]
        if step[0] == "prepare":
            queries, own, live, keep, bias = prepare(
                after(queries, *earlier), kv_pool, span_lengths, owner_branch, branch_table
            )
            marks["prepare"] = live
        elif step[0] == "attend":
            stage += 1
            pieces = held | {0: own}
            state = [
                attend_pieces(
                    queries, after(keep, *earlier), live, bias, pieces, step[1], state, stage == stages
                )
            ]
            if stage < stages:
                marks["attend%d" % stage] = state[0]
        else:
            number = step[1] ^ MOVES[step[0]]
            held[number] = permute(after(held[step[1]], *earlier), step[0])
            marks[number] = held[number]
    return state[0]


def attend_anywhere(queries, kv_pool, span_lengths, owner_branch, prefix_table, branch_table):
    device_count = lax.axis_size("seq")
    self_index = lax.axis_index("seq")
    owner_width = device_count // span_lengths.shape[0]
    branch = owner_branch[self_index // owner_width]
    live_count = span_lengths[branch] - self_index % owner_width * queries.shape[0]
    slot_branch = page_owners(prefix_table, branch_table, kv_pool.shape[0] * device_count)
    page_allowed = (slot_branch < 0) | (slot_branch == branch)
    return attend_general(queries, kv_pool, page_allowed, live_count)


def per_device(queries, kv_pool, span_lengths, owner_branch, prefix_table, branch_table):
    if lax.axis_size("seq") == GATHER_DEVICES and kv_pool.shape[1] == 8:
        return attend_staged(queries, kv_pool, span_lengths, owner_branch, branch_table)
    return attend_anywhere(
        queries, kv_pool, span_lengths, owner_branch, prefix_table, branch_table
    )


def solution(mesh):
    return jax.shard_map(
        per_device,
        mesh=mesh,
        in_specs=(
            P(("grp", "seq"), None),
            P(("grp", "seq"), None, None),
            P("grp"),
            P("grp"),
            P("grp"),
            P("grp", None),
        ),
        out_specs=P(("grp", "seq"), None),
        check_vma=False,
    )
```

```python
import functools
import math

import jax
import jax.numpy as jnp
from jax import lax
from jax.experimental import pallas as pl
from jax.experimental.pallas import tpu as pltpu
from jax.sharding import PartitionSpec as P

QH = 32
KVH = 4
HD = 128
GROUP = QH // KVH
EXP2_SCALE = math.log2(math.e) / math.sqrt(HD)
GATHER_DEVICES = 16
TOGETHER = 2
MASKED = -1e30


def page_owners(prefix_table, branch_table, pool_size):
    page_ids = jnp.arange(pool_size, dtype=jnp.int32)
    is_prefix = jnp.any(prefix_table[:, None] == page_ids[None, :], 0)
    flat_table = branch_table.reshape(-1)
    table_branch = jnp.arange(flat_table.shape[0], dtype=jnp.int32) // branch_table.shape[1]
    owner_of = jnp.sum(
        jnp.where(flat_table[:, None] == page_ids[None, :], table_branch[:, None], 0), 0
    )
    return jnp.where(is_prefix, -1, owner_of)


def absorb(carry, query_heads, pages, block_allowed):
    run_max, run_total, run_acc = carry
    page_tokens = pages.shape[1]
    token_count = pages.shape[0] * page_tokens
    kv_tokens = pages.reshape(token_count, 2, KVH, HD)
    keys = kv_tokens[:, 0]
    values = kv_tokens[:, 1]
    scores = jnp.einsum("rkgd,tkd->rkgt", query_heads, keys, preferred_element_type=jnp.float32) * (
        1.0 / math.sqrt(HD)
    )
    allowed = jnp.repeat(block_allowed, page_tokens)[None, None, None, :]
    masked = jnp.where(allowed, scores, -1e30)
    new_max = jnp.maximum(run_max, jnp.max(masked, -1))
    weights = jnp.where(allowed, jnp.exp(scores - new_max[..., None]), 0.0).astype(jnp.bfloat16)
    factor = jnp.exp(run_max - new_max)
    new_total = run_total * factor + jnp.sum(weights.astype(jnp.float32), -1)
    new_acc = run_acc * factor[..., None] + jnp.einsum(
        "rkgt,tkd->rkgd", weights, values, preferred_element_type=jnp.float32
    )
    return (new_max, new_total, new_acc)


def attend_general(queries, kv_pool, page_allowed, live_count):
    row_count = queries.shape[0]
    pages = lax.all_gather(kv_pool, "seq", axis=0, tiled=True)
    page_tokens = pages.shape[1]
    block_pages = max(1, max(128, 32768 // row_count) // page_tokens)
    while pages.shape[0] % block_pages:
        block_pages = block_pages - 1
    blocks = pages.reshape((-1, block_pages) + pages.shape[1:])
    block_allowed = page_allowed.reshape(-1, block_pages)
    query_heads = queries.reshape(row_count, KVH, GROUP, HD)
    start = (
        jnp.full((row_count, KVH, GROUP), -1e30, jnp.float32),
        jnp.zeros((row_count, KVH, GROUP), jnp.float32),
        jnp.zeros((row_count, KVH, GROUP, HD), jnp.float32),
    )

    def scan_step(state, inputs):
        block, allowed = inputs
        return (absorb(state, query_heads, block, allowed), None)

    (run_max, run_total, run_acc), unused = lax.scan(scan_step, start, (blocks, block_allowed))
    mixed = (run_acc / run_total[..., None]).reshape(row_count, QH * HD)
    live = jnp.arange(row_count, dtype=jnp.int32) < live_count
    return jnp.where(live[:, None], mixed, 0.0).astype(jnp.bfloat16)


MOVES = {"core": 1, "x": 2, "z1": 4, "z2": 8}
PLAN = (
    ("z2", 0, ()),
    ("z1", 0, ()),
    ("x", 0, ()),
    ("core", 0, ()),
    ("prepare", ()),
    ("x", 4, ("prepare",)),
    ("attend", (0, 4), ()),
    ("z1", 8, ("attend1",)),
    ("x", 8, ()),
    ("x", 12, ()),
    ("core", 2, ()),
    ("core", 4, ()),
    ("core", 6, ()),
    ("core", 8, ()),
    ("core", 10, ()),
    ("core", 12, ()),
    ("attend", (1, 2, 3, 5, 6, 7, 8), ()),
    ("core", 14, ("attend2",)),
    ("attend", (9, 10, 12, (13, 0, 5)), (14,)),
    ("attend", (11, (13, 5, 9), 14, 15), ()),
)


def permute(block, move):
    pairs = [(index, index ^ MOVES[move]) for index in range(GATHER_DEVICES)]
    return lax.ppermute(block, "seq", pairs)


def after(value, *earlier):
    return lax.optimization_barrier((value,) + earlier)[0] if earlier else value


def prepare_kernel(
    q_ref, shard_ref, lengths_in, owner_in, table_in, q_out, shard_out, live_ref, keep_ref, bias_ref, *rest
):
    lengths_ref, owner_ref, table_ref, sems = rest
    ends = (
        (lengths_in, lengths_ref),
        (owner_in, owner_ref),
        (table_in, table_ref),
        (q_ref, q_out),
        (shard_ref, shard_out),
    )
    copies = [pltpu.make_async_copy(*pair, sems.at[i]) for i, pair in enumerate(ends)]
    for copy in copies:
        copy.start()
    keep_ref[...] = jnp.ones(keep_ref.shape, jnp.float32)
    for copy in copies[:3]:
        copy.wait()
    pages_dev, page_tokens = shard_ref.shape[:2]
    piece_tokens = pages_dev * page_tokens
    me = lax.axis_index("seq")
    rows = q_ref.shape[0]
    owner_width = GATHER_DEVICES // owner_ref.shape[0]
    branch = owner_ref[me // owner_width]
    live_count = lengths_ref[branch] - me % owner_width * rows
    live_ref[...] = jnp.where(
        lax.broadcasted_iota(jnp.int32, live_ref.shape, 0) < live_count, 1.0, 0.0
    )
    entries = table_ref.shape[0]
    history = entries // owner_ref.shape[0]
    token = lax.broadcasted_iota(jnp.int32, bias_ref.shape, 1)
    bias = jnp.zeros(bias_ref.shape, jnp.float32)
    for e in range(entries):
        page = table_ref[e]
        device = page // pages_dev
        begin = (device ^ me) * piece_tokens + (page - device * pages_dev) * page_tokens
        seen = jnp.where(branch == e // history, 1.0, 0.0)
        rows_of_page = pl.ds(pl.multiple_of(begin, page_tokens), page_tokens)
        keep_ref[rows_of_page, :] = jnp.full((page_tokens, HD), seen, jnp.float32)
        in_page = (token >= begin) & (token < begin + page_tokens)
        bias = jnp.where(in_page, (1.0 - seen) * MASKED, bias)
    bias_ref[...] = bias
    for copy in copies[3:]:
        copy.wait()


def prepare(queries, shard, span_lengths, owner_branch, branch_table):
    vmem = pl.BlockSpec(memory_space=pltpu.VMEM)
    tables = (span_lengths, owner_branch, branch_table.reshape(-1))
    inputs = [
        pltpu.with_memory_space_constraint(value, pltpu.HBM) for value in (queries, shard) + tables
    ]
    tokens = GATHER_DEVICES * shard.shape[0] * shard.shape[1]
    shapes = [
        jax.ShapeDtypeStruct(queries.shape, queries.dtype),
        jax.ShapeDtypeStruct(shard.shape, shard.dtype),
        jax.ShapeDtypeStruct((queries.shape[0], HD), jnp.float32),
        jax.ShapeDtypeStruct((tokens, HD), jnp.float32),
        jax.ShapeDtypeStruct((1, tokens), jnp.float32),
    ]
    return pl.pallas_call(
        prepare_kernel,
        out_shape=shapes,
        in_specs=[pl.BlockSpec(memory_space=pltpu.HBM)] * len(inputs),
        out_specs=[vmem] * len(shapes),
        scratch_shapes=[pltpu.SMEM(table.shape, table.dtype) for table in tables]
        + [pltpu.SemaphoreType.DMA((len(inputs),))],
        compiler_params=pltpu.CompilerParams(vmem_limit_bytes=4 << 20),
        name="prepare",
    )(*inputs)


def part_of(entry, pages_dev):
    return (entry, 0, pages_dev) if isinstance(entry, int) else entry


def lay_out(piece_ref, begin, end, h, keep):
    tokens = (end - begin) * piece_ref.shape[1]
    keys = piece_ref[begin:end, :, h * HD : (h + 1) * HD].reshape(tokens, HD)
    values = piece_ref[begin:end, :, (KVH + h) * HD : (KVH + h + 1) * HD].reshape(tokens, HD)
    return keys, values * keep, keep


def stage_sums(q_ref, keep_ref, piece_refs, numbers, keys, values, old_sums, give):
    tokens = keys.shape[1]
    pages_dev, page_tokens = piece_refs[0].shape[:2]
    parts = [part_of(entry, pages_dev) for entry in numbers]
    held = sum(end - begin for _, begin, end in parts) * page_tokens
    if held < tokens:
        keys[:, held:, :] = jnp.zeros((KVH, tokens - held, HD), jnp.bfloat16)
        values[:, held:, :] = jnp.zeros((KVH, tokens - held, 2 * HD), jnp.bfloat16)
    filled = 0
    for i, (number, begin, end) in enumerate(parts):
        first = (number * pages_dev + begin) * page_tokens
        count = (end - begin) * page_tokens
        keep = keep_ref[first : first + count, :].astype(jnp.bfloat16)
        span = slice(filled, filled + count)
        filled += count
        for h in range(KVH):
            keys[h, span, :], values[h, span, :HD], values[h, span, HD:] = lay_out(
                piece_refs[i], begin, end, h, keep
            )
    rows = q_ref.shape[0]
    for begin in range(0, QH, TOGETHER):
        h = begin // GROUP
        heads = range(begin, begin + TOGETHER)
        q = jnp.concatenate([q_ref[:, n * HD : (n + 1) * HD] for n in heads], 0)
        scores = lax.dot_general(
            q, keys[h], (((1,), (1,)), ((), ())), preferred_element_type=jnp.float32
        )
        weights = jnp.exp2(scores * EXP2_SCALE).astype(jnp.bfloat16)
        sums = jnp.dot(weights, values[h], preferred_element_type=jnp.float32)
        for i, n in enumerate(heads):
            part = sums[i * rows : (i + 1) * rows]
            if old_sums is not None:
                part = part + old_sums[:, n * 2 * HD : (n + 1) * 2 * HD]
            give(n, part)


def stage_kernel(*refs, numbers, first):
    q_ref, keep_ref = refs[:2]
    piece_refs = refs[2 : 2 + len(numbers)]
    rest = list(refs[2 + len(numbers) :])
    old_sums = None if first else rest.pop(0)
    out_ref, keys, values = rest

    def give(n, part):
        out_ref[:, n * 2 * HD : (n + 1) * 2 * HD] = part

    stage_sums(q_ref, keep_ref, piece_refs, numbers, keys, values, old_sums, give)


def last_kernel(*refs, numbers):
    q_ref, keep_ref, live_ref, bias_ref = refs[:4]
    piece_refs = refs[4 : 4 + GATHER_DEVICES]
    old_sums, out_ref, keys, values, out_vmem, all_keys, all_values, sems = refs[4 + GATHER_DEVICES :]
    rows = q_ref.shape[0]
    live = live_ref[...] > 0.0
    chunk = GROUP * HD
    copies = [
        pltpu.make_async_copy(
            out_vmem.at[:, h * chunk : (h + 1) * chunk],
            out_ref.at[:, h * chunk : (h + 1) * chunk],
            sems.at[h],
        )
        for h in range(KVH)
    ]
    added = [jnp.zeros((rows, HD), jnp.float32), jnp.full((rows, HD), 1.0, jnp.float32)]

    def give(n, part):
        mixed, totals = part[:, :HD], part[:, HD:]
        added[0] = added[0] + totals
        added[1] = jnp.minimum(added[1], totals)
        inverse = pl.reciprocal(totals, approx=True)
        inverse = inverse * (2.0 - totals * inverse)
        lanes = slice(n * HD, (n + 1) * HD)
        out_vmem[:, lanes] = jnp.where(live, mixed * inverse, 0.0).astype(jnp.bfloat16)
        if n % GROUP == GROUP - 1:
            copies[n // GROUP].start()

    pages_dev = piece_refs[0].shape[0]
    new_refs = [piece_refs[part_of(entry, pages_dev)[0]] for entry in numbers]
    stage_sums(q_ref, keep_ref, new_refs, numbers, keys, values, old_sums, give)
    fits = (added[0] <= 2.0**100) & (added[1] >= 2.0**-100)
    fits = jnp.min(jnp.where(fits, 1.0, 0.0).reshape(rows // 8, 8, HD), 0)
    fits = jnp.min(fits)
    for copy in copies:
        copy.wait()

    @pl.when(fits < 0.5)
    def with_row_maxima():
        bias = bias_ref[...]
        piece_tokens = piece_refs[0].shape[0] * piece_refs[0].shape[1]
        for h in range(KVH):
            for number in range(GATHER_DEVICES):
                span = slice(number * piece_tokens, (number + 1) * piece_tokens)
                keep = keep_ref[span, :].astype(jnp.bfloat16)
                all_keys[span, :], all_values[span, :HD], all_values[span, HD:] = lay_out(
                    piece_refs[number], 0, pages_dev, h, keep
                )

            def one_head(g, unused):
                lanes = pl.ds(pl.multiple_of((h * GROUP + g) * HD, HD), HD)
                scores = lax.dot_general(
                    q_ref[:, lanes],
                    all_keys[...],
                    (((1,), (1,)), ((), ())),
                    preferred_element_type=jnp.float32,
                )
                scores = scores + bias
                row_max = jnp.max(scores, -1, keepdims=True)
                weights = jnp.exp2((scores - row_max) * EXP2_SCALE).astype(jnp.bfloat16)
                sums = jnp.dot(weights, all_values[...], preferred_element_type=jnp.float32)
                mixed = jnp.where(live, sums[:, :HD] / sums[:, HD:], 0.0)
                out_vmem[:, lanes] = mixed.astype(jnp.bfloat16)
                return unused

            lax.fori_loop(0, GROUP, one_head, 0)
        for copy in copies:
            copy.start()
        for copy in copies:
            copy.wait()


def attend_pieces(queries, keep, live, bias, pieces, numbers, state, last):
    rows, features = queries.shape
    pages_dev, page_tokens = pieces[0].shape[:2]
    parts = [part_of(entry, pages_dev) for entry in numbers]
    held = sum(end - begin for _, begin, end in parts) * page_tokens
    tokens = held + -held % HD
    vmem = pl.BlockSpec(memory_space=pltpu.VMEM)
    scratch = [
        pltpu.VMEM((KVH, tokens, HD), jnp.bfloat16),
        pltpu.VMEM((KVH, tokens, 2 * HD), jnp.bfloat16),
    ]
    if last:
        everything = GATHER_DEVICES * pages_dev * page_tokens
        scratch += [
            pltpu.VMEM((rows, features), jnp.bfloat16),
            pltpu.VMEM((everything, HD), jnp.bfloat16),
            pltpu.VMEM((everything, 2 * HD), jnp.bfloat16),
            pltpu.SemaphoreType.DMA((KVH,)),
        ]
        kernel = functools.partial(last_kernel, numbers=numbers)
        operands = [queries, keep, live, bias] + [pieces[n] for n in range(GATHER_DEVICES)]
        out_shape = jax.ShapeDtypeStruct((rows, features), jnp.bfloat16)
    else:
        kernel = functools.partial(stage_kernel, numbers=numbers, first=not state)
        operands = [queries, keep] + [pieces[n] for n, _, _ in parts]
        out_shape = jax.ShapeDtypeStruct((rows, 2 * features), jnp.float32)
    operands += state
    return pl.pallas_call(
        kernel,
        out_shape=out_shape,
        in_specs=[vmem] * len(operands),
        out_specs=pl.BlockSpec(memory_space=pltpu.HBM) if last else vmem,
        scratch_shapes=scratch,
        compiler_params=pltpu.CompilerParams(vmem_limit_bytes=24 << 20),
        cost_estimate=pl.CostEstimate(flops=0, bytes_accessed=0, transcendentals=0),
        name="attention_last" if last else "attention_stage",
    )(*operands)


def attend_staged(queries, kv_pool, span_lengths, owner_branch, branch_table):
    held = {0: kv_pool}
    marks = {}
    state, stage, stages = [], 0, sum(step[0] == "attend" for step in PLAN)
    for step in PLAN:
        earlier = [marks[name] for name in step[-1]]
        if step[0] == "prepare":
            queries, own, live, keep, bias = prepare(
                after(queries, *earlier), kv_pool, span_lengths, owner_branch, branch_table
            )
            marks["prepare"] = live
        elif step[0] == "attend":
            stage += 1
            pieces = held | {0: own}
            state = [
                attend_pieces(
                    queries, after(keep, *earlier), live, bias, pieces, step[1], state, stage == stages
                )
            ]
            if stage < stages:
                marks["attend%d" % stage] = state[0]
        else:
            number = step[1] ^ MOVES[step[0]]
            held[number] = permute(after(held[step[1]], *earlier), step[0])
            marks[number] = held[number]
    return state[0]


def attend_anywhere(queries, kv_pool, span_lengths, owner_branch, prefix_table, branch_table):
    device_count = lax.axis_size("seq")
    self_index = lax.axis_index("seq")
    owner_width = device_count // span_lengths.shape[0]
    branch = owner_branch[self_index // owner_width]
    live_count = span_lengths[branch] - self_index % owner_width * queries.shape[0]
    slot_branch = page_owners(prefix_table, branch_table, kv_pool.shape[0] * device_count)
    page_allowed = (slot_branch < 0) | (slot_branch == branch)
    return attend_general(queries, kv_pool, page_allowed, live_count)


def per_device(queries, kv_pool, span_lengths, owner_branch, prefix_table, branch_table):
    if lax.axis_size("seq") == GATHER_DEVICES and kv_pool.shape[1] == 8:
        return attend_staged(queries, kv_pool, span_lengths, owner_branch, branch_table)
    return attend_anywhere(
        queries, kv_pool, span_lengths, owner_branch, prefix_table, branch_table
    )


def solution(mesh):
    return jax.shard_map(
        per_device,
        mesh=mesh,
        in_specs=(
            P(("grp", "seq"), None),
            P(("grp", "seq"), None, None),
            P("grp"),
            P("grp"),
            P("grp"),
            P("grp", None),
        ),
        out_specs=P(("grp", "seq"), None),
        check_vma=False,
    )
```
